256 devices in a mesh: dp: 32 (over x, z), seq: 8 (over y, core).
Axes of the slice: x: 4, y: 4, z: 8, core: 2. Of those that a mesh axis runs over, the one named last changes fastest.
Arguments:
- query: bfloat16 [32768, 4096], P(('dp', 'seq')), may hold values from -64 to 64
- key_states: bfloat16 [32768, 1024], P(('dp', 'seq')), may hold values from -16 to 16
- value_states: bfloat16 [32768, 1024], P(('dp', 'seq')), may hold values from -6 to 6
- out_grad: bfloat16 [32768, 4096], P(('dp', 'seq')), may hold values from -6 to 6
- target_group: int32 [32768], P(('dp', 'seq')), may hold values from 0 to 31, as said below
- document: int32 [32768], P(('dp', 'seq')), may hold values from 0 to 1
Outputs:
- attention_out: bfloat16 [32768, 4096], P(('dp', 'seq'))
- query_grad: bfloat16 [32768, 4096], P(('dp', 'seq'))
- key_grad: bfloat16 [32768, 1024], P(('dp', 'seq'))
- value_grad: bfloat16 [32768, 1024], P(('dp', 'seq'))
The draws below stay inside these ranges and needn't reach their ends.
Inputs may be any that keep to these rules, and one draw needn't show every extreme that they name: `target_group`: the 128 rows of one device name each group at most 5 times. In every draw, for each index of seq, some group is named exactly 5 times by the rows of every device with that index of seq.
All inputs are finite; a program needn't handle non-finite values.
Results may differ from the reference program's by a relative error of at most 0.035.
Values may be sent and summed in bfloat16 or wider, within the bound.
A program may use at most 128 MiB of HBM per device.

```python
import math
import jax
import jax.numpy as jnp
import numpy as np
from jax import lax

HEADS = 32
KVH = 8
HD = 128
DOCS = 2
TOK_DEV = 128
CAP = 5
GROUP_SLOTS = 1280
TOKENS = 32768
N_DP = 32
N_SEQ = 8


def draw_query(key, part):
    key = jax.random.fold_in(key, 11)
    key_base = jax.random.fold_in(key, 0)
    values = jax.random.normal(key_base, (TOKENS, HEADS, HD), jnp.float32)
    values = jnp.clip(values, -64.0, 64.0)
    return values.reshape(TOKENS, HEADS * HD).astype(jnp.bfloat16)


def draw_key_states(key, part):
    key = jax.random.fold_in(key, 23)
    values = jax.random.normal(key, (TOKENS, KVH, HD), jnp.float32)
    values = jnp.clip(values, -16.0, 16.0)
    return values.reshape(TOKENS, KVH * HD).astype(jnp.bfloat16)


def draw_target_group(key, part):
    key = jax.random.fold_in(key, 5)
    key_full, key_score, key_perm = jax.random.split(key, 3)
    devices = N_DP * N_SEQ
    full_group = jax.random.randint(key_full, (N_SEQ,), 0, N_DP, dtype=jnp.int32)
    full_device = jnp.tile(full_group, N_DP)
    slot_ids = jnp.arange(N_DP * CAP, dtype=jnp.int32)
    slot_group = slot_ids // CAP
    scores = jax.random.randint(key_score, (devices, N_DP * CAP), 0, 2 ** 16, dtype=jnp.int32) * 8192 + slot_ids[None, :]
    scores = scores + jnp.where(slot_group[None, :] == full_device[:, None], 2 ** 29, 0).astype(jnp.int32)
    best_scores, chosen = lax.top_k(scores, TOK_DEV)
    groups = (chosen // CAP).astype(jnp.int32)
    groups = jax.random.permutation(key_perm, groups, axis=1, independent=True)
    return groups.reshape(TOKENS).astype(jnp.int32)


def with_ends(array, own_key, low, largest):
    longest = array.shape.index(max(array.shape))
    spots = []
    for shift in (0, 1):
        where = [jax.random.randint(jax.random.fold_in(own_key, axis), (), 0, length) for axis, length in enumerate(array.shape)]
        where[longest] = (where[longest] + shift) % array.shape[longest]
        spots.append(tuple(where))
    return array.at[spots[0]].set(low).at[spots[1]].set(largest)


def levels(key, extent, shards, low, high):
    def one(axis_at, blocks):
        steps = jax.random.uniform(jax.random.fold_in(jax.random.fold_in(key, 6), axis_at), (blocks,), jnp.float32, low / len(shards), high / len(shards))
        return jnp.repeat(jnp.exp(steps), extent[axis_at] // blocks).reshape((-1,) + (1,) * (len(extent) - axis_at - 1))

    gain = one(*shards[0])
    for cut in shards[1:]:
        gain = gain * one(*cut)
    return gain


def rank_table(count, slope):
    loads = [(1 << 20) // math.isqrt(rank ** slope) + 1 for rank in range(1, count + 1)]
    deviation = 1 + sum(loads) // (1 << 30)
    return np.cumsum(np.array([max(1, weight // deviation) for weight in loads]))


def skewed_ids(stream_key, extent, number_of, lean):
    table = rank_table(number_of, lean)
    pick = jax.random.randint(jax.random.fold_in(stream_key, 1), extent, 0, int(table[number_of - 1]))
    grade = jnp.searchsorted(jnp.asarray(table, jnp.int32), pick, side="right")
    return jax.random.permutation(jax.random.fold_in(stream_key, 2), number_of)[grade].astype(jnp.int32)


def bell_draw(stream_key, shape, width, reach, shards=(), held_as=jnp.bfloat16):
    values = jax.random.normal(stream_key, shape, jnp.float32) * width
    if len(shards) > 0:
        values = levels(stream_key, shape, shards, -0.22, 0.18) * values
    return jnp.clip(values, min=-reach, max=reach).astype(held_as)


def setup_inputs(seed: int = 0) -> dict:
    splits = jax.random.split(jax.random.key(seed), 7)
    return {
        "query": draw_query(jax.random.fold_in(splits[6], 71), 0),
        "key_states": draw_key_states(jax.random.fold_in(splits[6], 71), 0),
        "value_states": bell_draw(splits[2], (TOKENS, KVH * HD), 1.0, 6.0, ((0, 256),)),
        "out_grad": bell_draw(splits[3], (TOKENS, HEADS * HD), 1.0, 6.0, ((0, 256),)),
        "target_group": draw_target_group(jax.random.fold_in(splits[6], 71), 0),
        "document": with_ends(skewed_ids(splits[5], (TOKENS,), DOCS, 2), jax.random.fold_in(splits[5], 3), 0, DOCS - 1).astype(jnp.int32),
    }


def head_block(q_heads, k_head, v_head, g_heads, allowed, row_valid):
    inv_root = 1.0 / math.sqrt(HD)
    q_float = q_heads.astype(jnp.float32)
    k_float = k_head.astype(jnp.float32)
    v_float = v_head.astype(jnp.float32)
    g_float = g_heads.astype(jnp.float32)
    scores = jnp.einsum('rid,jd->rij', q_float, k_float) * inv_root
    scores = jnp.where(allowed[None], scores, -1e+30)
    row_max = lax.optimization_barrier(jnp.max(scores, axis=2, keepdims=True))
    exp_scores = jnp.where(allowed[None], jnp.exp(scores - row_max), 0.0)
    row_total = jnp.where(row_valid[None, :, None], lax.optimization_barrier(jnp.sum(exp_scores, axis=2, keepdims=True)), 1.0)
    probs_full = exp_scores / row_total
    probs_low = lax.optimization_barrier(probs_full.astype(jnp.bfloat16))
    attn_out = jnp.einsum('rij,jd->rid', probs_low.astype(jnp.float32), v_float).astype(jnp.bfloat16)
    attn_out = lax.optimization_barrier(attn_out)
    delta_row = lax.optimization_barrier(jnp.sum(g_float * attn_out.astype(jnp.float32), axis=2, keepdims=True))
    prob_grad = jnp.einsum('rid,jd->rij', g_float, v_float)
    score_grad = lax.optimization_barrier((probs_full * (prob_grad - delta_row)).astype(jnp.bfloat16))
    grad_float = score_grad.astype(jnp.float32)
    q_grad = (jnp.einsum('rij,jd->rid', grad_float, k_float) * inv_root).astype(jnp.bfloat16)
    k_grad = (jnp.einsum('rij,rid->jd', grad_float, q_float) * inv_root).astype(jnp.bfloat16)
    v_grad = jnp.einsum('rij,rid->jd', probs_low.astype(jnp.float32), g_float).astype(jnp.bfloat16)
    return (attn_out, q_grad, k_grad, v_grad)

def reference(query, key_states, value_states, out_grad, target_group, document):
    head_ratio = HEADS // KVH
    order_rows = jnp.argsort(target_group, stable=True).astype(jnp.int32)
    group_ids = jnp.arange(N_DP, dtype=jnp.int32)
    counts_all = lax.optimization_barrier(jnp.sum((target_group[None, :] == group_ids[:, None]).astype(jnp.int32), axis=1))
    starts = (jnp.cumsum(counts_all) - counts_all).astype(jnp.int32)

    def one_group(group_id):
        slot_line = jnp.arange(GROUP_SLOTS, dtype=jnp.int32)
        row_valid = slot_line < counts_all[group_id]
        where_at = jnp.clip(starts[group_id] + slot_line, 0, TOKENS - 1).astype(jnp.int32)
        picked = order_rows[where_at]
        doc_ids = jnp.where(row_valid, document[picked], -1)
        allowed = (doc_ids[:, None] == doc_ids[None, :]) & row_valid[:, None] & (picked[None, :] <= picked[:, None])
        q_heads = query[picked].reshape(GROUP_SLOTS, KVH, head_ratio, HD).transpose(1, 2, 0, 3)
        g_heads = out_grad[picked].reshape(GROUP_SLOTS, KVH, head_ratio, HD).transpose(1, 2, 0, 3)
        k_heads = key_states[picked].reshape(GROUP_SLOTS, KVH, HD).transpose(1, 0, 2)
        v_heads = value_states[picked].reshape(GROUP_SLOTS, KVH, HD).transpose(1, 0, 2)

        def per_head(pieces):
            return head_block(pieces[0], pieces[1], pieces[2], pieces[3], allowed, row_valid)
        attn_out, q_grad, k_grad, v_grad = lax.map(per_head, (q_heads, k_heads, v_heads, g_heads))
        attn_out = attn_out.transpose(2, 0, 1, 3).reshape(GROUP_SLOTS, HEADS * HD)
        q_grad = q_grad.transpose(2, 0, 1, 3).reshape(GROUP_SLOTS, HEADS * HD)
        k_grad = k_grad.transpose(1, 0, 2).reshape(GROUP_SLOTS, KVH * HD)
        v_grad = v_grad.transpose(1, 0, 2).reshape(GROUP_SLOTS, KVH * HD)
        target_rows = jnp.where(row_valid, picked, TOKENS).astype(jnp.int32)
        return (attn_out, q_grad, k_grad, v_grad, target_rows)
    results = lax.map(one_group, group_ids)
    target_rows = results[4].reshape(-1)

    def place_rows(values, row_width):
        empty = jnp.zeros((TOKENS, row_width), jnp.bfloat16)
        return empty.at[target_rows].set(values.reshape(-1, row_width), mode='drop')
    return (place_rows(results[0], HEADS * HD), place_rows(results[1], HEADS * HD), place_rows(results[2], KVH * HD), place_rows(results[3], KVH * HD))
```

```python
import math

import jax
import jax.numpy as jnp
from jax import lax
from jax.experimental import pallas as pl
from jax.experimental.pallas import tpu as pltpu
from jax.sharding import PartitionSpec as P

HD = 128
NX, NZ, NS = 4, 8, 8
NG = NX * NS
CAP = 5
SLOTS = NG * CAP
HALF = SLOTS // 2
KEYS = NZ * SLOTS
HEADS, KVH, RATIO = 32, 8, 4
UNITS = 16
PIECES = 4
ROWS = 128
BLK = 16
MESH = pl.DeviceIdType.MESH
BF16 = jnp.bfloat16
F32 = jnp.float32
VMEM_LIMIT = 56 * 1024 * 1024


def iota(shape, dim):
    return lax.broadcasted_iota(jnp.int32, shape, dim)


def dot(a, b):
    return lax.dot_general(a, b, (((1,), (0,)), ((), ())), preferred_element_type=F32)


def dot_nt(a, b):
    return lax.dot_general(a, b, (((1,), (1,)), ((), ())), preferred_element_type=F32)


def place():
    dp, seq = lax.axis_index("dp"), lax.axis_index("seq")
    return dp // NZ, lax.rem(dp, NZ), seq


def plane_device(x, z, seq, step):
    to_x = lax.rem(x + step // NS, NX)
    rest = lax.rem(step, NS)
    to_y = lax.rem(seq // 2 + rest // 2, NS // 2)
    to_core = lax.rem(seq + rest, 2)
    to_seq = to_y * 2 + to_core
    return to_x * NS + to_seq, (to_x * NZ + z, to_seq)


def swap_matrix():
    row, col = iota((256, 256), 0), iota((256, 256), 1)
    return (col == lax.rem(row, 16) * 16 + row // 16).astype(BF16)


def slot_rows(group_ref):
    across = jnp.broadcast_to(group_ref[...], (ROWS, ROWS)).astype(F32)
    down = across.T
    earlier = (across == down) & (iota((ROWS, ROWS), 0) < iota((ROWS, ROWS), 1))
    rank = jnp.sum(earlier.astype(F32), axis=0, keepdims=True)
    return across[:1] * CAP + rank


def slot_matrix(group_ref):
    return (iota((SLOTS, ROWS), 0).astype(F32) == slot_rows(group_ref)).astype(BF16)


def swap_tiles(swap, tiles):
    mixed = dot(swap, jnp.concatenate(tiles, axis=0)).astype(BF16)
    return [mixed[i * 16 : (i + 1) * 16] for i in range(16)]


def greet(x, z, seq, ring):
    barrier = pltpu.get_barrier_semaphore()

    def signal(step, carry):
        _, device = plane_device(x, z, seq, step)
        pl.semaphore_signal(barrier, inc=1, device_id=device, device_id_type=MESH)
        return carry

    lax.fori_loop(1, NG, signal, 0)
    for device in ring:
        pl.semaphore_signal(barrier, inc=1, device_id=device, device_id_type=MESH)
    pl.semaphore_wait(barrier, NG - 1 + len(ring))


def exchange_start(x, z, seq, send, recv, send_sem, recv_sem, own_sem):
    me = x * NS + seq

    def one(step, carry):
        to, device = plane_device(x, z, seq, step)
        pltpu.make_async_remote_copy(
            src_ref=send.at[to],
            dst_ref=recv.at[me],
            send_sem=send_sem,
            recv_sem=recv_sem,
            device_id=device,
            device_id_type=MESH,
        ).start()
        return carry

    lax.fori_loop(1, NG, one, 0)
    pltpu.make_async_copy(send.at[me], recv.at[me], own_sem).start()


def exchange_wait_recv(recv, recv_sem, own_sem):
    pltpu.make_async_copy(recv.at[pl.ds(0, NG - 1)], recv.at[pl.ds(0, NG - 1)], recv_sem).wait()
    pltpu.make_async_copy(recv.at[0], recv.at[0], own_sem).wait()


def exchange_wait_send(send, send_sem):
    pltpu.make_async_copy(send.at[pl.ds(0, NG - 1)], send.at[pl.ds(0, NG - 1)], send_sem).wait()


def token_tiles(ref, base, block):
    tiles = []
    for t in range(block * BLK, block * BLK + BLK):
        tiles.append(ref[base + (t // CAP,) + (t % CAP,)])
    return tiles


def put_tiles(ref, base, block, tiles):
    for i, tile in enumerate(tiles):
        t = block * BLK + i
        ref[base + (t // CAP,) + (t % CAP,)] = tile


def spread_kernel(
    q_ref, k_ref, v_ref, g_ref, group_ref, doc_ref,
    kv_ref, meta_ref, qu_ref, gu_ref,
    send0, recv0, send, recv,
    s0, r0, o0, ss, rs, os, ring_s, ring_r, meta_s, meta_r,
):
    x, z, seq = place()
    me = x * NS + seq
    right = (x * NZ + lax.rem(z + 1, NZ), seq)
    left = (x * NZ + lax.rem(z + NZ - 1, NZ), seq)

    pick = slot_matrix(group_ref)
    swap = swap_matrix()

    def pack(into, base, parts):
        packed = [dot(pick, part).astype(BF16) for part in parts]
        for block in range(SLOTS // BLK):
            rows = slice(block * BLK, (block + 1) * BLK)
            tiles = []
            for unit in range(UNITS):
                src, at = packed[unit // (UNITS // len(parts))], unit % (UNITS // len(parts))
                tiles.append(src[rows, at * HD : (at + 1) * HD])
            put_tiles(into, base, block, swap_tiles(swap, tiles))

    pack(send0, (), [k_ref[...], v_ref[...]])
    code = dot_nt(pick, jnp.broadcast_to(doc_ref[...] + 1, (HD, ROWS)).astype(BF16))
    slot, lane = iota((SLOTS, HD), 0), iota((SLOTS, HD), 1)
    at_lane = lax.rem(me, 2) * CAP + lax.rem(slot, CAP)
    code = jnp.where(lane == at_lane, code, 0.0).astype(BF16)
    row, col = iota((NG * 16, SLOTS), 0), iota((NG * 16, SLOTS), 1)
    sel = ((row // 16 == col // CAP) & (lax.rem(row, 16) == me // 2)).astype(BF16)
    codes = dot(sel, code).astype(BF16)
    for d in range(NG):
        send0[d, CAP] = codes[d * 16 : (d + 1) * 16]

    greet(x, z, seq, (left, right))
    exchange_start(x, z, seq, send0, recv0, s0, r0, o0)

    for piece in range(PIECES):
        cols = slice(piece * 1024, (piece + 1) * 1024)
        pack(send, (piece,), [q_ref[:, cols], g_ref[:, cols]])
        exchange_start(
            x, z, seq, send.at[piece], recv.at[piece], ss.at[piece], rs.at[piece], os.at[piece]
        )

    exchange_wait_recv(recv0, r0, o0)
    here = pl.multiple_of(z * HALF, BLK)
    for block in range(SLOTS // BLK):
        tiles = swap_tiles(swap, token_tiles(recv0, (), block))
        half, at = block // 5, (block % 5) * BLK
        for unit in range(UNITS):
            kv_ref[unit % 8, unit // 8, half, pl.ds(here + at, BLK), :] = tiles[unit]
    total = recv0[0, CAP]
    for s in range(1, NG):
        total = total + recv0[s, CAP]
    meta_ref[z] = total

    def ring_copy(lane_id, step):
        goes_right = lane_id < 2
        owner = lax.rem(z - step + NZ, NZ) if goes_right else lax.rem(z + step, NZ)
        block = kv_ref.at[
            pl.ds(lane_id * 2, 2), :, :, pl.ds(pl.multiple_of(owner * HALF, BLK), HALF), :
        ]
        return pltpu.make_async_remote_copy(
            src_ref=block,
            dst_ref=block,
            send_sem=ring_s.at[lane_id, step],
            recv_sem=ring_r.at[lane_id, step],
            device_id=right if goes_right else left,
            device_id_type=MESH,
        )

    def meta_copy(step):
        owner = lax.rem(z - step + NZ, NZ)
        return pltpu.make_async_remote_copy(
            src_ref=meta_ref.at[owner],
            dst_ref=meta_ref.at[owner],
            send_sem=meta_s.at[step],
            recv_sem=meta_r.at[step],
            device_id=right,
            device_id_type=MESH,
        )

    def unpack(piece):
        exchange_wait_recv(recv.at[piece], rs.at[piece], os.at[piece])
        for block in range(SLOTS // BLK):
            tiles = swap_tiles(swap, token_tiles(recv, (piece,), block))
            rows = slice(block * BLK, (block + 1) * BLK)
            for unit in range(8):
                qu_ref[piece * 8 + unit, rows, :] = tiles[unit]
                gu_ref[piece * 8 + unit, rows, :] = tiles[8 + unit]

    for step in range(NZ - 1):
        for lane_id in (0, 2, 1, 3):
            if step > 0:
                ring_copy(lane_id, step - 1).wait_recv()
            ring_copy(lane_id, step).start()
        if step > 0:
            meta_copy(step - 1).wait_recv()
        meta_copy(step).start()
        if step >= 3:
            unpack(step - 3)
    for lane_id in range(4):
        ring_copy(lane_id, NZ - 2).wait_recv()
    meta_copy(NZ - 2).wait_recv()
    for step in range(NZ - 1):
        for lane_id in range(4):
            ring_copy(lane_id, step).wait_send()
        meta_copy(step).wait_send()
    exchange_wait_send(send0, s0)
    for piece in range(PIECES):
        exchange_wait_send(send.at[piece], ss.at[piece])


LANES = RATIO * SLOTS
SPLIT = 256


def mask_bias(meta_ref, bias):
    _, z, _ = place()
    t, b16 = iota((SLOTS, 16), 0), iota((SLOTS, 16), 1)
    spread = (t // 10 == b16).astype(BF16)
    t2, lane = iota((SLOTS, HD), 0), iota((SLOTS, HD), 1)
    ones = jnp.ones((HD, HD), BF16)
    lane_q = iota((HD, LANES), 1)
    tq = (lane_q // (RATIO * HALF)) * HALF + lax.rem(lane_q, HALF)
    expand = (iota((HD, LANES), 0) == lax.rem(tq, 10)).astype(BF16)
    wide = dot(meta_ref[z], expand)
    lane_q = iota((16, LANES), 1)
    tq = (lane_q // (RATIO * HALF)) * HALF + lax.rem(lane_q, HALF)
    code_q = jnp.sum(jnp.where(iota((16, LANES), 0) == tq // 10, wide, 0.0), axis=0, keepdims=True)
    tq = tq[:1]
    order_q = (tq // 40) * 320 + z * 40 + lax.rem(tq, 40)
    for zk in range(NZ):
        picked = dot(spread, meta_ref[zk])
        picked = jnp.where(lane == lax.rem(t2, 10), picked, 0.0).astype(BF16)
        code_k = dot(picked, ones)
        order_k = (t2 // 40) * 320 + zk * 40 + lax.rem(t2, 40)
        for half in range(2):
            rows = slice(half * HALF, (half + 1) * HALF)
            for at in range(0, LANES, HD):
                cols = slice(at, at + HD)
                ok = (
                    (code_k[rows] == code_q[:, cols])
                    & (code_k[rows] > 0.5)
                    & (order_k[rows] <= order_q[:, cols])
                )
                bias[pl.ds(half * NZ * HALF + zk * HALF, HALF), cols] = jnp.where(ok, 0.0, -1e30)


def attend_kernel(kv_ref, meta_ref, q_ref, g_ref, o_ref, dq_ref, dkv_ref, bias, p_ref, ds_ref):
    inv_root = 1.0 / math.sqrt(HD)
    log_scale = inv_root * math.log2(math.e)

    @pl.when(pl.program_id(0) == 0)
    def _():
        mask_bias(meta_ref, bias)

    def rows_of(ref):
        return jnp.concatenate(
            [ref[h, half * HALF : (half + 1) * HALF, :] for half in range(2) for h in range(RATIO)],
            axis=0,
        )

    q, g = rows_of(q_ref), rows_of(g_ref)
    k = kv_ref[0, 0].reshape(KEYS, HD)
    v = kv_ref[0, 1].reshape(KEYS, HD)
    kt, vt, gt = k.T, v.T, g.T
    outs, dqs = [], []
    for lo, hi, n in ((0, SPLIT, KEYS // 2), (SPLIT, 2 * SPLIT, KEYS), (2 * SPLIT, LANES, KEYS)):
        s = dot_nt(k[:n], q[lo:hi]) * log_scale + bias[:n, lo:hi]
        p = jnp.exp2(s - jnp.max(s, axis=0, keepdims=True))
        p = p * (1.0 / jnp.sum(p, axis=0, keepdims=True))
        low = p.astype(BF16)
        p_ref[:n, lo:hi] = low
        out = dot(vt[:, :n], low).astype(BF16)
        delta = jnp.sum(gt[:, lo:hi].astype(F32) * out.astype(F32), axis=0, keepdims=True)
        ds = (p * (dot_nt(v[:n], g[lo:hi]) - delta)).astype(BF16)
        ds_ref[:n, lo:hi] = ds
        outs.append(out.T)
        dqs.append((dot(kt[:, :n], ds) * inv_root).astype(BF16).T)
    out, dq = jnp.concatenate(outs, axis=0), jnp.concatenate(dqs, axis=0)
    for half in range(2):
        for h in range(RATIO):
            rows = slice((half * RATIO + h) * HALF, (half * RATIO + h + 1) * HALF)
            o_ref[h, half * HALF : (half + 1) * HALF, :] = out[rows]
            dq_ref[h, half * HALF : (half + 1) * HALF, :] = dq[rows]
    n = KEYS // 2
    for half, lo in ((0, 0), (1, SPLIT)):
        rows = slice(half * n, (half + 1) * n)
        dkv_ref[0, 0, half] = (dot(ds_ref[rows, lo:], q[lo:]) * inv_root).astype(BF16)
        dkv_ref[0, 1, half] = dot(p_ref[rows, lo:], g[lo:]).astype(BF16)


def collect_kernel(
    o_ref, dq_ref, dkv_ref, group_ref,
    out_ref, qg_ref, kg_ref, vg_ref,
    send0, recv0, send, recv, land, stage,
    s0, r0, o0, ss, rs, os, ring_s, ring_r,
):
    x, z, seq = place()
    right = (x * NZ + lax.rem(z + 1, NZ), seq)
    left = (x * NZ + lax.rem(z + NZ - 1, NZ), seq)
    pick_t = slot_matrix(group_ref).astype(F32).T.astype(BF16)
    swap = swap_matrix()
    greet(x, z, seq, (left, right))

    def own(lane_id, step):
        goes_right = lane_id < 2
        to = lax.rem(z - 1 - step + 2 * NZ, NZ) if goes_right else lax.rem(z + 1 + step, NZ)
        return dkv_ref[
            pl.ds(lane_id * 2, 2), :, :, pl.ds(pl.multiple_of(to * HALF, BLK), HALF), :
        ]

    def ring_copy(lane_id, step):
        return pltpu.make_async_remote_copy(
            src_ref=stage.at[lane_id, step],
            dst_ref=land.at[lane_id, step],
            send_sem=ring_s.at[lane_id, step],
            recv_sem=ring_r.at[lane_id, step],
            device_id=right if lane_id < 2 else left,
            device_id_type=MESH,
        )

    def summed(lane_id, step):
        return (
            own(lane_id, step).astype(F32) + land[lane_id, step - 1].astype(F32)
        ).astype(BF16)

    def pack(piece):
        for block in range(SLOTS // BLK):
            rows = slice(block * BLK, (block + 1) * BLK)
            tiles = [o_ref[piece * 8 + unit, rows, :] for unit in range(8)]
            tiles += [dq_ref[piece * 8 + unit, rows, :] for unit in range(8)]
            put_tiles(send, (piece,), block, swap_tiles(swap, tiles))
        exchange_start(
            x, z, seq, send.at[piece], recv.at[piece], ss.at[piece], rs.at[piece], os.at[piece]
        )

    def unpack(ref, base, outs):
        parts = [[] for _ in range(UNITS)]
        for block in range(SLOTS // BLK):
            tiles = swap_tiles(swap, token_tiles(ref, base, block))
            for unit in range(UNITS):
                parts[unit].append(tiles[unit])
        for unit in range(UNITS):
            rows = jnp.concatenate(parts[unit], axis=0)
            target, at = outs[unit // 8], unit % 8
            target[:, at * HD : (at + 1) * HD] = dot(pick_t, rows).astype(BF16)

    for step in range(NZ - 1):
        for lane_id in (0, 2, 1, 3):
            if step > 0:
                ring_copy(lane_id, step - 1).wait_recv()
                stage[lane_id, step] = summed(lane_id, step)
            else:
                stage[lane_id, step] = own(lane_id, step)
            ring_copy(lane_id, step).start()
        if step < PIECES:
            pack(step)
    for lane_id in range(4):
        ring_copy(lane_id, NZ - 2).wait_recv()
        stage[lane_id, NZ - 1] = summed(lane_id, NZ - 1)
    for block in range(SLOTS // BLK):
        half, at = block // 5, (block % 5) * BLK
        tiles = []
        for unit in range(UNITS):
            head, which = unit % 8, unit // 8
            tiles.append(stage[head // 2, NZ - 1, head % 2, which, half, at : at + BLK, :])
        put_tiles(send0, (), block, swap_tiles(swap, tiles))
    exchange_start(x, z, seq, send0, recv0, s0, r0, o0)
    for piece in range(PIECES):
        exchange_wait_recv(recv.at[piece], rs.at[piece], os.at[piece])
        cols = pl.ds(piece * 1024, 1024)
        unpack(recv, (piece,), [out_ref.at[:, cols], qg_ref.at[:, cols]])
    exchange_wait_recv(recv0, r0, o0)
    unpack(recv0, (), [kg_ref, vg_ref])
    for step in range(NZ - 1):
        for lane_id in range(4):
            ring_copy(lane_id, step).wait_send()
    exchange_wait_send(send0, s0)
    for piece in range(PIECES):
        exchange_wait_send(send.at[piece], ss.at[piece])


def per_device(query, key_states, value_states, out_grad, target_group, document):
    vmem = pl.BlockSpec(memory_space=pltpu.VMEM)
    dma = pltpu.SemaphoreType.DMA
    group = target_group.reshape(1, ROWS)
    doc = document.reshape(1, ROWS)
    kv_shape = (KVH, 2, 2, NZ * HALF, HD)
    kv, meta, qu, gu = pl.pallas_call(
        spread_kernel,
        out_shape=[
            jax.ShapeDtypeStruct(kv_shape, BF16),
            jax.ShapeDtypeStruct((NZ, 16, HD), BF16),
            jax.ShapeDtypeStruct((HEADS, SLOTS, HD), BF16),
            jax.ShapeDtypeStruct((HEADS, SLOTS, HD), BF16),
        ],
        in_specs=[vmem] * 6,
        out_specs=[vmem] * 4,
        scratch_shapes=[
            pltpu.VMEM((NG, CAP + 1, UNITS, HD), BF16),
            pltpu.VMEM((NG, CAP + 1, UNITS, HD), BF16),
            pltpu.VMEM((PIECES, NG, CAP, UNITS, HD), BF16),
            pltpu.VMEM((PIECES, NG, CAP, UNITS, HD), BF16),
            dma, dma, dma,
            dma((PIECES,)), dma((PIECES,)), dma((PIECES,)),
            dma((4, NZ - 1)), dma((4, NZ - 1)),
            dma((NZ - 1,)), dma((NZ - 1,)),
        ],
        compiler_params=pltpu.CompilerParams(
            collective_id=0, has_side_effects=True, vmem_limit_bytes=VMEM_LIMIT
        ),
        name="spread",
    )(query, key_states, value_states, out_grad, group, doc)

    heads = pl.BlockSpec((RATIO, SLOTS, HD), lambda c: (c, 0, 0))
    kv_block = pl.BlockSpec((1, 2, 2, NZ * HALF, HD), lambda c: (c, 0, 0, 0, 0))
    out, dq, dkv = pl.pallas_call(
        attend_kernel,
        grid=(KVH,),
        out_shape=[
            jax.ShapeDtypeStruct((HEADS, SLOTS, HD), BF16),
            jax.ShapeDtypeStruct((HEADS, SLOTS, HD), BF16),
            jax.ShapeDtypeStruct(kv_shape, BF16),
        ],
        in_specs=[kv_block, pl.BlockSpec((NZ, 16, HD), lambda c: (0, 0, 0)), heads, heads],
        out_specs=[heads, heads, kv_block],
        scratch_shapes=[
            pltpu.VMEM((KEYS, LANES), F32),
            pltpu.VMEM((KEYS, LANES), BF16),
            pltpu.VMEM((KEYS, LANES), BF16),
        ],
        compiler_params=pltpu.CompilerParams(vmem_limit_bytes=VMEM_LIMIT),
        name="attend",
    )(kv, meta, qu, gu)

    return tuple(
        pl.pallas_call(
            collect_kernel,
            out_shape=[
                jax.ShapeDtypeStruct((ROWS, HEADS * HD), BF16),
                jax.ShapeDtypeStruct((ROWS, HEADS * HD), BF16),
                jax.ShapeDtypeStruct((ROWS, KVH * HD), BF16),
                jax.ShapeDtypeStruct((ROWS, KVH * HD), BF16),
            ],
            in_specs=[vmem] * 4,
            out_specs=[vmem] * 4,
            scratch_shapes=[
                pltpu.VMEM((NG, CAP, UNITS, HD), BF16),
                pltpu.VMEM((NG, CAP, UNITS, HD), BF16),
                pltpu.VMEM((PIECES, NG, CAP, UNITS, HD), BF16),
                pltpu.VMEM((PIECES, NG, CAP, UNITS, HD), BF16),
                pltpu.VMEM((4, NZ - 1, 2, 2, 2, HALF, HD), BF16),
                pltpu.VMEM((4, NZ, 2, 2, 2, HALF, HD), BF16),
                dma, dma, dma,
                dma((PIECES,)), dma((PIECES,)), dma((PIECES,)),
                dma((4, NZ - 1)), dma((4, NZ - 1)),
            ],
            compiler_params=pltpu.CompilerParams(
                collective_id=1, has_side_effects=True, vmem_limit_bytes=VMEM_LIMIT
            ),
            name="collect",
        )(out, dq, dkv, group)
    )


def solution(mesh):
    rows = P(("dp", "seq"), None)
    line = P(("dp", "seq"))
    return jax.shard_map(
        per_device,
        mesh=mesh,
        in_specs=(rows, rows, rows, rows, line, line),
        out_specs=(rows, rows, rows, rows),
        check_vma=False,
    )
```

```python
import math

import jax
import jax.numpy as jnp
from jax import lax
from jax.experimental import pallas as pl
from jax.experimental.pallas import tpu as pltpu
from jax.sharding import PartitionSpec as P

HD = 128
NX, NZ, NS = 4, 8, 8
NG = NX * NS
CAP = 5
SLOTS = NG * CAP
HALF = SLOTS // 2
KEYS = NZ * SLOTS
HEADS, KVH, RATIO = 32, 8, 4
UNITS = 16
PIECES = 4
ROWS = 128
BLK = 16
MESH = pl.DeviceIdType.MESH
BF16 = jnp.bfloat16
F32 = jnp.float32
VMEM_LIMIT = 56 * 1024 * 1024


def iota(shape, dim):
    return lax.broadcasted_iota(jnp.int32, shape, dim)


def dot(a, b):
    return lax.dot_general(a, b, (((1,), (0,)), ((), ())), preferred_element_type=F32)


def dot_nt(a, b):
    return lax.dot_general(a, b, (((1,), (1,)), ((), ())), preferred_element_type=F32)


def place():
    dp, seq = lax.axis_index("dp"), lax.axis_index("seq")
    return dp // NZ, lax.rem(dp, NZ), seq


def plane_device(x, z, seq, step):
    to_x = lax.rem(x + step // NS, NX)
    rest = lax.rem(step, NS)
    to_y = lax.rem(seq // 2 + rest // 2, NS // 2)
    to_core = lax.rem(seq + rest, 2)
    to_seq = to_y * 2 + to_core
    return to_x * NS + to_seq, (to_x * NZ + z, to_seq)


def swap_matrix():
    row, col = iota((256, 256), 0), iota((256, 256), 1)
    return (col == lax.rem(row, 16) * 16 + row // 16).astype(BF16)


def slot_rows(group_ref):
    across = jnp.broadcast_to(group_ref[...], (ROWS, ROWS)).astype(F32)
    down = across.T
    earlier = (across == down) & (iota((ROWS, ROWS), 0) < iota((ROWS, ROWS), 1))
    rank = jnp.sum(earlier.astype(F32), axis=0, keepdims=True)
    return across[:1] * CAP + rank


def slot_matrix(group_ref):
    return (iota((SLOTS, ROWS), 0).astype(F32) == slot_rows(group_ref)).astype(BF16)


def swap_tiles(swap, tiles):
    mixed = dot(swap, jnp.concatenate(tiles, axis=0)).astype(BF16)
    return [mixed[i * 16 : (i + 1) * 16] for i in range(16)]


def greet(x, z, seq, ring):
    barrier = pltpu.get_barrier_semaphore()

    def signal(step, carry):
        _, device = plane_device(x, z, seq, step)
        pl.semaphore_signal(barrier, inc=1, device_id=device, device_id_type=MESH)
        return carry

    lax.fori_loop(1, NG, signal, 0)
    for device in ring:
        pl.semaphore_signal(barrier, inc=1, device_id=device, device_id_type=MESH)
    pl.semaphore_wait(barrier, NG - 1 + len(ring))


def exchange_start(x, z, seq, send, recv, send_sem, recv_sem, own_sem):
    me = x * NS + seq

    def one(step, carry):
        to, device = plane_device(x, z, seq, step)
        pltpu.make_async_remote_copy(
            src_ref=send.at[to],
            dst_ref=recv.at[me],
            send_sem=send_sem,
            recv_sem=recv_sem,
            device_id=device,
            device_id_type=MESH,
        ).start()
        return carry

    lax.fori_loop(1, NG, one, 0)
    pltpu.make_async_copy(send.at[me], recv.at[me], own_sem).start()


def exchange_wait_recv(recv, recv_sem, own_sem):
    pltpu.make_async_copy(recv.at[pl.ds(0, NG - 1)], recv.at[pl.ds(0, NG - 1)], recv_sem).wait()
    pltpu.make_async_copy(recv.at[0], recv.at[0], own_sem).wait()


def exchange_wait_send(send, send_sem):
    pltpu.make_async_copy(send.at[pl.ds(0, NG - 1)], send.at[pl.ds(0, NG - 1)], send_sem).wait()


def token_tiles(ref, base, block):
    tiles = []
    for t in range(block * BLK, block * BLK + BLK):
        tiles.append(ref[base + (t // CAP,) + (t % CAP,)])
    return tiles


def put_tiles(ref, base, block, tiles):
    for i, tile in enumerate(tiles):
        t = block * BLK + i
        ref[base + (t // CAP,) + (t % CAP,)] = tile


LANES = RATIO * SLOTS
SPLIT = 256
SET = KVH // 2
INV_ROOT = 1.0 / math.sqrt(HD)


def query_slots(rows):
    lane = iota((rows, LANES), 1)
    return (lane // (RATIO * HALF)) * HALF + lax.rem(lane, HALF)


def query_codes(meta):
    expand = (iota((HD, LANES), 0) == lax.rem(query_slots(HD), 10)).astype(BF16)
    own = iota((16, LANES), 0) == query_slots(16) // 10
    return jnp.sum(jnp.where(own, dot(meta, expand), 0.0), axis=0, keepdims=True)


def mask_block(meta_ref, bias, z, zk):
    tq = query_slots(1)
    code_q = query_codes(meta_ref[z])
    order_q = (tq // 40) * 320 + z * 40 + lax.rem(tq, 40)
    slot, lane = iota((SLOTS, HD), 0), iota((SLOTS, HD), 1)
    spread = (iota((SLOTS, 16), 0) // 10 == iota((SLOTS, 16), 1)).astype(BF16)
    picked = jnp.where(lane == lax.rem(slot, 10), dot(spread, meta_ref[zk]), 0.0).astype(BF16)
    code_k = dot(picked, jnp.ones((HD, HD), BF16))
    order_k = (slot // 40) * 320 + zk * 40 + lax.rem(slot, 40)
    for half in range(2):
        rows = slice(half * HALF, (half + 1) * HALF)
        at_row = pl.multiple_of(half * NZ * HALF + zk * HALF, BLK)
        for at in range(0, LANES, HD):
            cols = slice(at, at + HD)
            ok = (
                (code_k[rows] == code_q[:, cols])
                & (code_k[rows] > 0.5)
                & (order_k[rows] <= order_q[:, cols])
            )
            bias[pl.ds(at_row, HALF), cols] = jnp.where(ok, 0.0, -1e30)


def attend_head(c, kv_ref, q_ref, g_ref, o_ref, dq_ref, dkv_ref, bias, p_ref, ds_ref, between):
    log_scale = INV_ROOT * math.log2(math.e)

    def rows_of(ref):
        return jnp.concatenate(
            [
                ref[c * RATIO + h, half * HALF : (half + 1) * HALF, :]
                for half in range(2)
                for h in range(RATIO)
            ],
            axis=0,
        )

    q, g = rows_of(q_ref), rows_of(g_ref)
    k = kv_ref[c, 0].reshape(KEYS, HD)
    v = kv_ref[c, 1].reshape(KEYS, HD)
    kt, vt, gt = k.T, v.T, g.T
    outs, dqs = [], []
    blocks = ((0, SPLIT, KEYS // 2), (SPLIT, 2 * SPLIT, KEYS), (2 * SPLIT, LANES, KEYS))
    for i, (lo, hi, n) in enumerate(blocks):
        s = dot_nt(k[:n], q[lo:hi]) * log_scale + bias[:n, lo:hi]
        p = jnp.exp2(s - jnp.max(s, axis=0, keepdims=True))
        p = p * (1.0 / jnp.sum(p, axis=0, keepdims=True))
        low = p.astype(BF16)
        p_ref[:n, lo:hi] = low
        out = dot(vt[:, :n], low).astype(BF16)
        delta = jnp.sum(gt[:, lo:hi].astype(F32) * out.astype(F32), axis=0, keepdims=True)
        ds = (p * (dot_nt(v[:n], g[lo:hi]) - delta)).astype(BF16)
        ds_ref[:n, lo:hi] = ds
        outs.append(out.T)
        dqs.append((dot(kt[:, :n], ds) * INV_ROOT).astype(BF16).T)
        between(i)
    out, dq = jnp.concatenate(outs, axis=0), jnp.concatenate(dqs, axis=0)
    for half in range(2):
        for h in range(RATIO):
            rows = slice((half * RATIO + h) * HALF, (half * RATIO + h + 1) * HALF)
            o_ref[c * RATIO + h, half * HALF : (half + 1) * HALF, :] = out[rows]
            dq_ref[c * RATIO + h, half * HALF : (half + 1) * HALF, :] = dq[rows]
    n = KEYS // 2
    for half, lo in ((0, 0), (1, SPLIT)):
        rows = slice(half * n, (half + 1) * n)
        dkv_ref[c, 0, half] = (dot(ds_ref[rows, lo:], q[lo:]) * INV_ROOT).astype(BF16)
        dkv_ref[c, 1, half] = dot(p_ref[rows, lo:], g[lo:]).astype(BF16)
    between(3)


def whole_kernel(
    q_ref, k_ref, v_ref, g_ref, group_ref, doc_ref,
    out_ref, qg_ref, kg_ref, vg_ref,
    kv_ref, meta_ref, qu_ref, gu_ref, ou_ref, dqu_ref, dkv_ref,
    bias, p_ref, ds_ref,
    send0, recv0, send, recv, dkv_send, back0, back, land,
    kv_s, kv_r, kv_o, row_s, row_r, row_o, dkv_s, dkv_r, dkv_o, res_s, res_r, res_o,
    ring_s, ring_r, sum_s, sum_r, meta_s, meta_r,
):
    x, z, seq = place()
    me = x * NS + seq
    right = (x * NZ + lax.rem(z + 1, NZ), seq)
    left = (x * NZ + lax.rem(z + NZ - 1, NZ), seq)

    pick = slot_matrix(group_ref)
    swap = swap_matrix()

    def pack_rows(into, base, parts):
        packed = [dot(pick, part).astype(BF16) for part in parts]
        for block in range(SLOTS // BLK):
            rows = slice(block * BLK, (block + 1) * BLK)
            tiles = []
            for unit in range(UNITS):
                src, at = packed[unit // 8], unit % 8
                tiles.append(src[rows, at * HD : (at + 1) * HD])
            put_tiles(into, base, block, swap_tiles(swap, tiles))

    def rows_start(piece):
        exchange_start(
            x, z, seq, send.at[piece], recv.at[piece],
            row_s.at[piece], row_r.at[piece], row_o.at[piece],
        )

    def rows_unpack(piece):
        exchange_wait_recv(recv.at[piece], row_r.at[piece], row_o.at[piece])
        for block in range(SLOTS // BLK):
            tiles = swap_tiles(swap, token_tiles(recv, (piece,), block))
            rows = slice(block * BLK, (block + 1) * BLK)
            for unit in range(8):
                qu_ref[piece * 8 + unit, rows, :] = tiles[unit]
                gu_ref[piece * 8 + unit, rows, :] = tiles[8 + unit]

    def results_start(piece):
        exchange_wait_send(send.at[piece], row_s.at[piece])
        for block in range(SLOTS // BLK):
            rows = slice(block * BLK, (block + 1) * BLK)
            tiles = [ou_ref[piece * 8 + unit, rows, :] for unit in range(8)]
            tiles += [dqu_ref[piece * 8 + unit, rows, :] for unit in range(8)]
            put_tiles(send, (piece,), block, swap_tiles(swap, tiles))
        exchange_start(
            x, z, seq, send.at[piece], back.at[piece],
            res_s.at[piece], res_r.at[piece], res_o.at[piece],
        )

    def unpack_back(ref, base, outs):
        parts = [[] for _ in range(UNITS)]
        for block in range(SLOTS // BLK):
            tiles = swap_tiles(swap, token_tiles(ref, base, block))
            for unit in range(UNITS):
                parts[unit].append(tiles[unit])
        for unit in range(UNITS):
            rows = jnp.concatenate(parts[unit], axis=0)
            target, at = outs[unit // 8], unit % 8
            target[:, at * HD : (at + 1) * HD] = dot(pick_t, rows).astype(BF16)

    def results_unpack(piece):
        exchange_wait_recv(back.at[piece], res_r.at[piece], res_o.at[piece])
        cols = pl.ds(piece * 1024, 1024)
        unpack_back(back, (piece,), [out_ref.at[:, cols], qg_ref.at[:, cols]])

    def plane(index):
        return pl.ds(pl.multiple_of(index * HALF, BLK), HALF)

    def gather_copy(first, lane, step):
        owner = lax.rem(z - step + NZ, NZ) if lane < 2 else lax.rem(z + step, NZ)
        block = kv_ref.at[first + lane, :, :, plane(owner), :]
        return pltpu.make_async_remote_copy(
            src_ref=block,
            dst_ref=block,
            send_sem=ring_s.at[first + lane, step],
            recv_sem=ring_r.at[first + lane, step],
            device_id=right if lane < 2 else left,
            device_id_type=MESH,
        )

    def meta_copy(step):
        owner = lax.rem(z - step + NZ, NZ)
        return pltpu.make_async_remote_copy(
            src_ref=meta_ref.at[owner],
            dst_ref=meta_ref.at[owner],
            send_sem=meta_s.at[step],
            recv_sem=meta_r.at[step],
            device_id=right,
            device_id_type=MESH,
        )

    def own_terms(lane, step):
        return plane(lax.rem(z - 1 - step + 2 * NZ, NZ) if lane < 2 else lax.rem(z + 1 + step, NZ))

    def sum_copy(first, lane, step, src):
        return pltpu.make_async_remote_copy(
            src_ref=src,
            dst_ref=land.at[first + lane, step],
            send_sem=sum_s.at[first + lane, step],
            recv_sem=sum_r.at[first + lane, step],
            device_id=right if lane < 2 else left,
            device_id_type=MESH,
        )

    def sum_first(first):
        for lane in (0, 2, 1, 3):
            src = dkv_ref.at[first + lane, :, :, own_terms(lane, 0), :]
            sum_copy(first, lane, 0, src).start()

    def sum_next(first, lane, step, send_on):
        slot = land.at[first + lane, step - 1]
        sum_copy(first, lane, step - 1, slot).wait_recv()
        own = dkv_ref[first + lane, :, :, own_terms(lane, step), :]
        slot[...] = (own.astype(F32) + slot[...].astype(F32)).astype(BF16)
        if send_on:
            sum_copy(first, lane, step, slot).start()

    pack_rows(send0, (), [k_ref[...], v_ref[...]])
    code = dot_nt(pick, jnp.broadcast_to(doc_ref[...] + 1, (HD, ROWS)).astype(BF16))
    slot, lane = iota((SLOTS, HD), 0), iota((SLOTS, HD), 1)
    code = jnp.where(lane == lax.rem(me, 2) * CAP + lax.rem(slot, CAP), code, 0.0).astype(BF16)
    row, col = iota((NG * 16, SLOTS), 0), iota((NG * 16, SLOTS), 1)
    sel = ((row // 16 == col // CAP) & (lax.rem(row, 16) == me // 2)).astype(BF16)
    codes = dot(sel, code).astype(BF16)
    for d in range(NG):
        send0[d, CAP] = codes[d * 16 : (d + 1) * 16]

    greet(x, z, seq, (left, right))
    exchange_start(x, z, seq, send0, recv0, kv_s, kv_r, kv_o)
    for piece in range(PIECES):
        cols = slice(piece * 1024, (piece + 1) * 1024)
        pack_rows(send, (piece,), [q_ref[:, cols], g_ref[:, cols]])

    exchange_wait_recv(recv0, kv_r, kv_o)
    here = pl.multiple_of(z * HALF, BLK)
    for block in range(SLOTS // BLK):
        tiles = swap_tiles(swap, token_tiles(recv0, (), block))
        half, at = block // 5, (block % 5) * BLK
        for unit in range(UNITS):
            kv_ref[unit % 8, unit // 8, half, pl.ds(here + at, BLK), :] = tiles[unit]
    total = recv0[0, CAP]
    for s in range(1, NG):
        total = total + recv0[s, CAP]
    meta_ref[z] = total

    for step in range(NZ - 1):
        for lane in (0, 2, 1, 3):
            if step > 0:
                gather_copy(0, lane, step - 1).wait_recv()
            gather_copy(0, lane, step).start()
        if step > 0:
            meta_copy(step - 1).wait_recv()
        meta_copy(step).start()
        if step < PIECES:
            rows_start(step)
        mask_block(meta_ref, bias, z, lax.rem(z - step + NZ, NZ))
        if step >= 5:
            rows_unpack(step - 5)
    for lane in (0, 2, 1, 3):
        gather_copy(SET, lane, 0).start()
    meta_copy(NZ - 2).wait_recv()
    mask_block(meta_ref, bias, z, lax.rem(z + 1, NZ))
    for lane in (0, 2, 1, 3):
        gather_copy(0, lane, NZ - 2).wait_recv()

    refs = (kv_ref, qu_ref, gu_ref, ou_ref, dqu_ref, dkv_ref, bias, p_ref, ds_ref)

    def first_heads(i, carry):
        def between(at):
            step = 2 * i + 1 + at // 2
            for lane in ((0, 2), (1, 3))[at % 2]:

                @pl.when(step < NZ)
                def _():
                    gather_copy(SET, lane, step - 1).wait_recv()

                @pl.when(step < NZ - 1)
                def _():
                    gather_copy(SET, lane, step).start()

        attend_head(i, *refs, between)
        return carry

    lax.fori_loop(0, SET, first_heads, 0)
    sum_first(0)
    for piece in (0, 1):
        results_start(piece)
    for piece in (2, 3):
        rows_unpack(piece)

    def other_heads(i, carry):
        def between(at):
            step = 2 * i + 1 + at // 2
            for lane in ((0, 2), (1, 3))[at % 2]:

                @pl.when(step < NZ - 1)
                def _():
                    sum_next(0, lane, step, True)

                @pl.when(step == NZ - 1)
                def _():
                    sum_next(0, lane, step, False)

        attend_head(i + SET, *refs, between)
        return carry

    lax.fori_loop(0, SET, other_heads, 0)
    sum_first(SET)
    for piece in (2, 3):
        results_start(piece)
    pick_t = pick.astype(F32).T.astype(BF16)
    for step in range(1, NZ):
        for lane in (0, 2, 1, 3):
            sum_next(SET, lane, step, step < NZ - 1)
        if step in (2, 4):
            results_unpack(step // 2 - 1)
    for block in range(SLOTS // BLK):
        half, at = block // 5, (block % 5) * BLK
        tiles = [
            land[unit % 8, NZ - 2, unit // 8, half, at : at + BLK, :] for unit in range(UNITS)
        ]
        for i, tile in enumerate(swap_tiles(swap, tiles)):
            t = block * BLK + i
            dkv_send[t // CAP, t % CAP] = tile
    exchange_start(x, z, seq, dkv_send, back0, dkv_s, dkv_r, dkv_o)
    for piece in (2, 3):
        results_unpack(piece)
    exchange_wait_recv(back0, dkv_r, dkv_o)
    unpack_back(back0, (), [kg_ref, vg_ref])

    for step in range(NZ - 1):
        for lane in range(4):
            for first in (0, SET):
                gather_copy(first, lane, step).wait_send()
                sum_copy(first, lane, step, land.at[first + lane, step]).wait_send()
        meta_copy(step).wait_send()
    exchange_wait_send(send0, kv_s)
    exchange_wait_send(dkv_send, dkv_s)
    for piece in range(PIECES):
        exchange_wait_send(send.at[piece], res_s.at[piece])


def per_device(query, key_states, value_states, out_grad, target_group, document):
    vmem = pl.BlockSpec(memory_space=pltpu.VMEM)
    dma = pltpu.SemaphoreType.DMA
    group = target_group.reshape(1, ROWS)
    doc = document.reshape(1, ROWS)
    kv_shape = (KVH, 2, 2, NZ * HALF, HD)
    heads_shape = (HEADS, SLOTS, HD)
    piece_shape = (PIECES, NG, CAP, UNITS, HD)
    result = pl.pallas_call(
        whole_kernel,
        out_shape=[
            jax.ShapeDtypeStruct((ROWS, HEADS * HD), BF16),
            jax.ShapeDtypeStruct((ROWS, HEADS * HD), BF16),
            jax.ShapeDtypeStruct((ROWS, KVH * HD), BF16),
            jax.ShapeDtypeStruct((ROWS, KVH * HD), BF16),
        ],
        in_specs=[vmem] * 6,
        out_specs=[vmem] * 4,
        scratch_shapes=[
            pltpu.VMEM(kv_shape, BF16),
            pltpu.VMEM((NZ, 16, HD), BF16),
            pltpu.VMEM(heads_shape, BF16),
            pltpu.VMEM(heads_shape, BF16),
            pltpu.VMEM(heads_shape, BF16),
            pltpu.VMEM(heads_shape, BF16),
            pltpu.VMEM(kv_shape, BF16),
            pltpu.VMEM((KEYS, LANES), F32),
            pltpu.VMEM((KEYS, LANES), BF16),
            pltpu.VMEM((KEYS, LANES), BF16),
            pltpu.VMEM((NG, CAP + 1, UNITS, HD), BF16),
            pltpu.VMEM((NG, CAP + 1, UNITS, HD), BF16),
            pltpu.VMEM(piece_shape, BF16),
            pltpu.VMEM(piece_shape, BF16),
            pltpu.VMEM((NG, CAP, UNITS, HD), BF16),
            pltpu.VMEM((NG, CAP, UNITS, HD), BF16),
            pltpu.VMEM(piece_shape, BF16),
            pltpu.VMEM((KVH, NZ - 1, 2, 2, HALF, HD), BF16),
            dma, dma, dma,
            dma((PIECES,)), dma((PIECES,)), dma((PIECES,)),
            dma, dma, dma,
            dma((PIECES,)), dma((PIECES,)), dma((PIECES,)),
            dma((KVH, NZ - 1)), dma((KVH, NZ - 1)),
            dma((KVH, NZ - 1)), dma((KVH, NZ - 1)),
            dma((NZ - 1,)), dma((NZ - 1,)),
        ],
        compiler_params=pltpu.CompilerParams(
            collective_id=0, has_side_effects=True, vmem_limit_bytes=VMEM_LIMIT
        ),
        name="whole",
    )(query, key_states, value_states, out_grad, group, doc)
    return tuple(result)


def solution(mesh):
    rows = P(("dp", "seq"), None)
    line = P(("dp", "seq"))
    return jax.shard_map(
        per_device,
        mesh=mesh,
        in_specs=(rows, rows, rows, rows, line, line),
        out_specs=(rows, rows, rows, rows),
        check_vma=False,
    )
```

```python
import math

import jax
import jax.numpy as jnp
from jax import lax
from jax.experimental import pallas as pl
from jax.experimental.pallas import tpu as pltpu
from jax.sharding import PartitionSpec as P

HD = 128
NX, NZ, NS = 4, 8, 8
NG = NX * NS
CAP = 5
SLOTS = NG * CAP
HALF = SLOTS // 2
KEYS = NZ * SLOTS
HEADS, KVH, RATIO = 32, 8, 4
UNITS = 16
PIECES = 4
ROWS = 128
BLK = 16
SET = KVH // 2
SETS = 2
WIDE = 8
LANES = RATIO * SLOTS
SPLIT = 256
INV_ROOT = 1.0 / math.sqrt(HD)
MESH = pl.DeviceIdType.MESH
BF16 = jnp.bfloat16
F32 = jnp.float32
VMEM_LIMIT = 56 * 1024 * 1024


def iota(shape, dim):
    return lax.broadcasted_iota(jnp.int32, shape, dim)


def dot(a, b):
    return lax.dot_general(a, b, (((1,), (0,)), ((), ())), preferred_element_type=F32)


def dot_nt(a, b):
    return lax.dot_general(a, b, (((1,), (1,)), ((), ())), preferred_element_type=F32)


def place():
    dp, seq = lax.axis_index("dp"), lax.axis_index("seq")
    return dp // NZ, lax.rem(dp, NZ), seq


def plane_device(x, z, seq, step):
    to_x = lax.rem(x + step // NS, NX)
    rest = lax.rem(step, NS)
    to_y = lax.rem(seq // 2 + rest // 2, NS // 2)
    to_core = lax.rem(seq + rest, 2)
    to_seq = to_y * 2 + to_core
    return to_x * NS + to_seq, (to_x * NZ + z, to_seq)


def slot_matrix(group_ref, width):
    across = jnp.broadcast_to(group_ref[...], (ROWS, ROWS)).astype(F32)
    down = across.T
    earlier = (across == down) & (iota((ROWS, ROWS), 0) < iota((ROWS, ROWS), 1))
    rank = jnp.sum(earlier.astype(F32), axis=0, keepdims=True)
    slot = across[:1] * width + rank
    return (iota((NG * width, ROWS), 0).astype(F32) == slot).astype(BF16)


def transposed(matrix):
    return matrix.astype(F32).T.astype(BF16)


def swap_tiles(swap, tiles):
    mixed = dot(swap, jnp.concatenate(tiles, axis=0)).astype(BF16)
    return [mixed[i * 16 : (i + 1) * 16] for i in range(mixed.shape[0] // 16)]


def greet(x, z, seq, ring):
    barrier = pltpu.get_barrier_semaphore()

    def signal(step, carry):
        _, device = plane_device(x, z, seq, step)
        pl.semaphore_signal(barrier, inc=1, device_id=device, device_id_type=MESH)
        return carry

    for device in ring:
        pl.semaphore_signal(barrier, inc=1, device_id=device, device_id_type=MESH)
    lax.fori_loop(1, NG, signal, 0)
    return barrier


def exchange_start(x, z, seq, send, recv, send_sem, recv_sem, own_sem):
    me = x * NS + seq

    def one(step, carry):
        to, device = plane_device(x, z, seq, step)
        pltpu.make_async_remote_copy(
            src_ref=send.at[to],
            dst_ref=recv.at[me],
            send_sem=send_sem,
            recv_sem=recv_sem,
            device_id=device,
            device_id_type=MESH,
        ).start()
        return carry

    lax.fori_loop(1, NG, one, 0)
    pltpu.make_async_copy(send.at[me], recv.at[me], own_sem).start()


def exchange_wait_recv(recv, recv_sem, own_sem):
    pltpu.make_async_copy(recv.at[pl.ds(0, NG - 1)], recv.at[pl.ds(0, NG - 1)], recv_sem).wait()
    pltpu.make_async_copy(recv.at[0], recv.at[0], own_sem).wait()


def exchange_wait_send(send, send_sem):
    pltpu.make_async_copy(send.at[pl.ds(0, NG - 1)], send.at[pl.ds(0, NG - 1)], send_sem).wait()


def token_tiles(ref, piece, block):
    return [ref[piece, t // CAP, t % CAP] for t in range(block * BLK, block * BLK + BLK)]


def put_tiles(ref, piece, block, tiles):
    for i, tile in enumerate(tiles):
        t = block * BLK + i
        ref[piece, t // CAP, t % CAP] = tile


def message_from_wide():
    out, src = iota((192, 256), 0), iota((192, 256), 1)
    group, row, unit = out // 48, lax.rem(out, 48) // 8, lax.rem(out, 8)
    return (src == unit * 32 + group * 8 + row).astype(BF16)


def units_from_message(block):
    out, src = iota((128, 192), 0), iota((128, 192), 1)
    slot = block * BLK + lax.rem(out, BLK) - first_message(block) * CAP
    return (src == (slot // CAP) * 48 + lax.rem(slot, CAP) * 8 + out // BLK).astype(BF16)


def first_message(block):
    return block * BLK // CAP


def message_from_units(four):
    out, src = iota((192, 256), 0), iota((192, 256), 1)
    row, unit = lax.rem(out, 48) // 8, lax.rem(out, 8)
    slot = four * 4 * CAP + (out // 48) * CAP + row - (four * 4 * CAP // BLK) * BLK
    return ((src == unit * 32 + slot) & (row < CAP)).astype(BF16)


def query_slots(rows):
    lane = iota((rows, LANES), 1)
    return (lane // (RATIO * HALF)) * HALF + lax.rem(lane, HALF)


def query_codes(meta):
    expand = (iota((HD, LANES), 0) == lax.rem(query_slots(HD), 20)).astype(BF16)
    own = iota((16, LANES), 0) == 8 + query_slots(16) // 20
    return jnp.sum(jnp.where(own, dot(meta, expand), 0.0), axis=0, keepdims=True)


def mask_block(meta_ref, bias, z, zk):
    tq = query_slots(1)
    code_q = query_codes(meta_ref[z])
    order_q = (tq // 40) * 320 + z * 40 + lax.rem(tq, 40)
    slot, lane = iota((SLOTS, HD), 0), iota((SLOTS, HD), 1)
    spread = (8 + iota((SLOTS, 16), 0) // 20 == iota((SLOTS, 16), 1)).astype(BF16)
    picked = jnp.where(lane == lax.rem(slot, 20), dot(spread, meta_ref[zk]), 0.0).astype(BF16)
    code_k = dot(picked, jnp.ones((HD, HD), BF16))
    order_k = (slot // 40) * 320 + zk * 40 + lax.rem(slot, 40)
    for half in range(2):
        rows = slice(half * HALF, (half + 1) * HALF)
        at_row = pl.multiple_of(half * NZ * HALF + zk * HALF, BLK)
        for at in range(0, LANES, HD):
            cols = slice(at, at + HD)
            ok = (
                (code_k[rows] == code_q[:, cols])
                & (code_k[rows] > 0.5)
                & (order_k[rows] <= order_q[:, cols])
            )
            bias[pl.ds(at_row, HALF), cols] = jnp.where(ok, 0.0, -1e30)


def attend_head(
    c, kv_ref, q_ref, g_ref, o_ref, dq_ref, dkv_ref, bias, p_ref, ds_ref, between
):
    log_scale = INV_ROOT * math.log2(math.e)

    def rows_of(ref):
        return jnp.concatenate(
            [
                ref[c * RATIO + h, half * HALF : (half + 1) * HALF, :]
                for half in range(2)
                for h in range(RATIO)
            ],
            axis=0,
        )

    q, g = rows_of(q_ref), rows_of(g_ref)
    k = kv_ref[c, 0].reshape(KEYS, HD)
    v = kv_ref[c, 1].reshape(KEYS, HD)
    kt, vt, gt = k.T, v.T, g.T
    outs, dqs = [], []
    blocks = ((0, SPLIT, KEYS // 2), (SPLIT, 2 * SPLIT, KEYS), (2 * SPLIT, LANES, KEYS))
    for i, (lo, hi, n) in enumerate(blocks):
        s = dot_nt(k[:n], q[lo:hi]) * log_scale + bias[:n, lo:hi]
        p = jnp.exp2(s - jnp.max(s, axis=0, keepdims=True))
        p = p * (1.0 / jnp.sum(p, axis=0, keepdims=True))
        low = p.astype(BF16)
        p_ref[:n, lo:hi] = low
        between(2 * i)
        out = dot(vt[:, :n], low).astype(BF16)
        delta = jnp.sum(gt[:, lo:hi].astype(F32) * out.astype(F32), axis=0, keepdims=True)
        ds = (p * (dot_nt(v[:n], g[lo:hi]) - delta)).astype(BF16)
        ds_ref[:n, lo:hi] = ds
        outs.append(out.T)
        dqs.append((dot(kt[:, :n], ds) * INV_ROOT).astype(BF16).T)
        between(2 * i + 1)
    out, dq = jnp.concatenate(outs, axis=0), jnp.concatenate(dqs, axis=0)
    for half in range(2):
        for h in range(RATIO):
            rows = slice((half * RATIO + h) * HALF, (half * RATIO + h + 1) * HALF)
            o_ref[c * RATIO + h, half * HALF : (half + 1) * HALF, :] = out[rows]
            dq_ref[c * RATIO + h, half * HALF : (half + 1) * HALF, :] = dq[rows]
    n = KEYS // 2
    for half, lo in ((0, 0), (1, SPLIT)):
        rows = slice(half * n, (half + 1) * n)
        dkv_ref[c, 0, half] = (dot(ds_ref[rows, lo:], q[lo:]) * INV_ROOT).astype(BF16)
        dkv_ref[c, 1, half] = dot(p_ref[rows, lo:], g[lo:]).astype(BF16)
        between(6 + half)


def whole_kernel(
    q_ref, k_ref, v_ref, g_ref, group_ref, doc_ref,
    out_ref, qg_ref, kg_ref, vg_ref,
    kv_ref, meta_ref, qu_ref, gu_ref, ou_ref, dqu_ref, dkv_ref,
    bias, p_ref, ds_ref,
    send0, recv0, send, recv, dkv_send, back0, back, land,
    kv_s, kv_r, kv_o, row_s, row_r, row_o, dkv_s, dkv_r, dkv_o, res_s, res_r, res_o,
    ring_s, ring_r, sum_s, sum_r, meta_s, meta_r,
):
    x, z, seq = place()
    me = x * NS + seq
    right = (x * NZ + lax.rem(z + 1, NZ), seq)
    left = (x * NZ + lax.rem(z + NZ - 1, NZ), seq)
    barrier = greet(x, z, seq, (left, right))

    pick = slot_matrix(group_ref, CAP)
    pick_wide = slot_matrix(group_ref, WIDE)
    row, col = iota((256, 256), 0), iota((256, 256), 1)
    swap = (col == lax.rem(row, 16) * 16 + row // 16).astype(BF16)

    def rows_pack(piece):
        cols = slice(piece * 1024, (piece + 1) * 1024)
        packed = [dot(pick, part[:, cols]).astype(BF16) for part in (q_ref, g_ref)]
        for block in range(SLOTS // BLK):
            rows = slice(block * BLK, (block + 1) * BLK)
            tiles = [part[rows, at * HD : (at + 1) * HD] for part in packed for at in range(8)]
            put_tiles(send, piece, block, swap_tiles(swap, tiles))

    def rows_start(piece):
        exchange_start(
            x, z, seq, send.at[piece], recv.at[piece],
            row_s.at[piece], row_r.at[piece], row_o.at[piece],
        )

    def rows_unpack(piece):
        exchange_wait_recv(recv.at[piece], row_r.at[piece], row_o.at[piece])
        for block in range(SLOTS // BLK):
            tiles = swap_tiles(swap, token_tiles(recv, piece, block))
            rows = slice(block * BLK, (block + 1) * BLK)
            for unit in range(8):
                qu_ref[piece * 8 + unit, rows, :] = tiles[unit]
                gu_ref[piece * 8 + unit, rows, :] = tiles[8 + unit]

    def results_start(piece):
        exchange_wait_send(send.at[piece], row_s.at[piece])
        for block in range(SLOTS // BLK):
            rows = slice(block * BLK, (block + 1) * BLK)
            tiles = [ou_ref[piece * 8 + unit, rows, :] for unit in range(8)]
            tiles += [dqu_ref[piece * 8 + unit, rows, :] for unit in range(8)]
            put_tiles(send, piece, block, swap_tiles(swap, tiles))
        exchange_start(
            x, z, seq, send.at[piece], back.at[piece],
            res_s.at[piece], res_r.at[piece], res_o.at[piece],
        )

    def results_unpack(piece):
        exchange_wait_recv(back.at[piece], res_r.at[piece], res_o.at[piece])
        pick_t = transposed(pick)
        parts = [[] for _ in range(UNITS)]
        for block in range(SLOTS // BLK):
            tiles = swap_tiles(swap, token_tiles(back, piece, block))
            for unit in range(UNITS):
                parts[unit].append(tiles[unit])
        for unit in range(UNITS):
            rows = jnp.concatenate(parts[unit], axis=0)
            at = (piece * 8 + unit % 8) * HD
            (out_ref, qg_ref)[unit // 8][:, at : at + HD] = dot(pick_t, rows).astype(BF16)

    def keys_pack(part, extra, mix):
        packed = []
        for unit in range(8):
            at = (part * SET + unit // 2) * HD
            rows = dot(pick_wide, (k_ref, v_ref)[unit % 2][:, at : at + HD])
            if extra is not None:
                rows = rows + jnp.where(me // 4 == unit, extra, 0.0)
            packed.append(rows.astype(BF16))
        for four in range(NG // 4):
            rows = slice(four * 32, (four + 1) * 32)
            tiles = swap_tiles(mix, [part_rows[rows] for part_rows in packed])
            for i, tile in enumerate(tiles):
                send0[part, four * 4 + i // 3, i % 3] = tile

    def keys_start(part):
        exchange_start(
            x, z, seq, send0.at[part], recv0.at[part],
            kv_s.at[part], kv_r.at[part], kv_o.at[part],
        )

    def keys_unpack(part):
        exchange_wait_recv(recv0.at[part], kv_r.at[part], kv_o.at[part])
        here = pl.multiple_of(z * HALF, BLK)
        for block in range(SLOTS // BLK):
            first = first_message(block)
            tiles = [recv0[part, first + i // 3, i % 3] for i in range(12)]
            tiles = swap_tiles(units_from_message(block), tiles)
            half, at = block // 5, (block % 5) * BLK
            for unit in range(8):
                kv_ref[part * SET + unit // 2, unit % 2, half, pl.ds(here + at, BLK), :] = tiles[
                    unit
                ]

    def terms_start(part):
        for four in range(NG // 4):
            lo = four * 4 * CAP // BLK * BLK
            tiles = []
            for unit in range(8):
                for at in (lo, lo + BLK):
                    half, in_half = at // HALF, at % HALF
                    tiles.append(
                        land[part * SET + unit // 2, unit % 2, NZ - 2, half, in_half : in_half + BLK, :]
                    )
            tiles = swap_tiles(message_from_units(four), tiles)
            for i, tile in enumerate(tiles):
                dkv_send[part, four * 4 + i // 3, i % 3] = tile
        exchange_start(
            x, z, seq, dkv_send.at[part], back0.at[part],
            dkv_s.at[part], dkv_r.at[part], dkv_o.at[part],
        )

    def terms_unpack(part):
        exchange_wait_recv(back0.at[part], dkv_r.at[part], dkv_o.at[part])
        pick_t = transposed(pick_wide)
        mix = transposed(message_from_wide())
        parts = [[] for _ in range(8)]
        for four in range(NG // 4):
            tiles = [back0[part, four * 4 + i // 3, i % 3] for i in range(12)]
            tiles = swap_tiles(mix, tiles)
            for unit in range(8):
                parts[unit] += tiles[2 * unit : 2 * unit + 2]
        for unit in range(8):
            rows = jnp.concatenate(parts[unit], axis=0)
            at = (part * SET + unit // 2) * HD
            (kg_ref, vg_ref)[unit % 2][:, at : at + HD] = dot(pick_t, rows).astype(BF16)

    def plane(index):
        return pl.ds(pl.multiple_of(index * HALF, BLK), HALF)

    def way(head):
        return 1 + lax.rem(head, 2) * (NZ - 2)

    def neighbour(head):
        return (x * NZ + lax.rem(z + way(head), NZ), seq)

    def gather_copy(head, which, step):
        owner = lax.rem(z + (NZ - way(head)) * step, NZ)
        block = kv_ref.at[head, which, :, plane(owner), :]
        return pltpu.make_async_remote_copy(
            src_ref=block,
            dst_ref=block,
            send_sem=ring_s.at[head, which, step],
            recv_sem=ring_r.at[head, which, step],
            device_id=neighbour(head),
            device_id_type=MESH,
        )

    def meta_copy(step):
        owner = lax.rem(z - step + NZ, NZ)
        return pltpu.make_async_remote_copy(
            src_ref=meta_ref.at[owner],
            dst_ref=meta_ref.at[owner],
            send_sem=meta_s.at[step],
            recv_sem=meta_r.at[step],
            device_id=right,
            device_id_type=MESH,
        )

    def terms_for(head, step):
        return plane(lax.rem(z + (NZ - way(head)) * (step + 1), NZ))

    def sum_copy(head, which, step, src):
        return pltpu.make_async_remote_copy(
            src_ref=src,
            dst_ref=land.at[head, which, step],
            send_sem=sum_s.at[head, which, step],
            recv_sem=sum_r.at[head, which, step],
            device_id=neighbour(head),
            device_id_type=MESH,
        )

    def sum_first(head):
        for which in range(2):
            src = dkv_ref.at[head, which, :, terms_for(head, 0), :]
            sum_copy(head, which, 0, src).start()

    def sum_next(head, which, step):
        slot = land.at[head, which, step - 1]
        sum_copy(head, which, step - 1, slot).wait_recv()
        own = dkv_ref[head, which, :, terms_for(head, step), :]
        slot[...] = (own.astype(F32) + slot[...].astype(F32)).astype(BF16)

        def send_on():
            sum_copy(head, which, step, slot).start()

        if isinstance(step, int):
            if step < NZ - 1:
                send_on()
        else:
            pl.when(step < NZ - 1)(send_on)

    code = dot_nt(pick_wide, jnp.broadcast_to(doc_ref[...] + 1, (HD, ROWS)).astype(BF16))
    slot, lane = iota((256, HD), 0), iota((256, HD), 1)
    code = jnp.where(lane == lax.rem(me, 4) * CAP + lax.rem(slot, WIDE), code, 0.0).astype(BF16)
    sel = ((row // WIDE == col // WIDE) & (lax.rem(row, WIDE) == CAP)).astype(BF16)
    mix = message_from_wide()
    keys_pack(0, dot(sel, code), mix)
    pl.semaphore_wait(barrier, NG + 1)
    keys_start(0)
    keys_pack(1, None, mix)
    keys_start(1)
    for piece in range(PIECES):
        rows_pack(piece)

    keys_unpack(0)
    total = recv0[0, 0, 2]
    for s in range(1, NG):
        total = total + recv0[0, s, 2]
    meta_ref[z] = total

    heads = (0, 1, 2, 3)
    for step in range(NZ - 1):
        for which in range(2):
            for head in heads:
                if step > 0:
                    gather_copy(head, which, step - 1).wait_recv()
                gather_copy(head, which, step).start()
        if step > 0:
            meta_copy(step - 1).wait_recv()
        meta_copy(step).start()
        if step < PIECES:
            rows_start(step)
        mask_block(meta_ref, bias, z, lax.rem(z - step + NZ, NZ))
        if step == 4:
            keys_unpack(1)
        if step >= 5:
            rows_unpack(step - 5)
    for which in range(2):
        for head in heads:
            gather_copy(SET + head, which, 0).start()
    meta_copy(NZ - 2).wait_recv()
    mask_block(meta_ref, bias, z, lax.rem(z + 1, NZ))
    for which in range(2):
        for head in heads:
            gather_copy(head, which, NZ - 2).wait_recv()

    refs = (kv_ref, qu_ref, gu_ref, ou_ref, dqu_ref, dkv_ref, bias, p_ref, ds_ref)

    def first_heads(i, carry):
        def between(at):
            step = 2 * i + 1 + at // 4
            which = (at % 4) // 2
            for head in ((0, 1), (2, 3))[at % 2]:

                @pl.when(step < NZ)
                def _():
                    gather_copy(SET + head, which, step - 1).wait_recv()

                @pl.when(step < NZ - 1)
                def _():
                    gather_copy(SET + head, which, step).start()

        attend_head(i, *refs, between)
        sum_first(i)

        @pl.when(lax.rem(i, 2) == 1)
        def _():
            results_start(i // 2)

        @pl.when(i >= 2)
        def _():
            rows_unpack(i)

        return carry

    lax.fori_loop(0, SET, first_heads, 0)

    def other_heads(i, carry):
        def between(at):
            step = 2 * i + 1 + at // 4
            which = (at % 4) // 2
            for head in ((0, 1), (2, 3))[at % 2]:

                @pl.when(step < NZ)
                def _():
                    sum_next(head, which, step)

        attend_head(i + SET, *refs, between)
        sum_first(i + SET)

        @pl.when(lax.rem(i, 2) == 1)
        def _():
            results_start(2 + i // 2)

        return carry

    lax.fori_loop(0, SET, other_heads, 0)
    for step in range(1, NZ):
        for which in range(2):
            for head in heads:
                sum_next(SET + head, which, step)
        if step == 1:
            terms_start(0)
        if step in (3, 4):
            results_unpack(step - 3)
        if step == 6:
            terms_unpack(0)
    terms_start(1)
    for piece in (2, 3):
        results_unpack(piece)
    terms_unpack(1)

    for step in range(NZ - 1):
        for which in range(2):
            for head in range(KVH):
                gather_copy(head, which, step).wait_send()
                sum_copy(head, which, step, land.at[head, which, step]).wait_send()
        meta_copy(step).wait_send()
    for part in range(SETS):
        exchange_wait_send(send0.at[part], kv_s.at[part])
        exchange_wait_send(dkv_send.at[part], dkv_s.at[part])
    for piece in range(PIECES):
        exchange_wait_send(send.at[piece], res_s.at[piece])


def copy_kernel(*refs):
    for src, dst in zip(refs[:4], refs[4:]):
        dst[...] = src[...]


def per_device(query, key_states, value_states, out_grad, target_group, document):
    vmem = pl.BlockSpec(memory_space=pltpu.VMEM)
    blocks = [pl.BlockSpec((ROWS // 4, heads * HD), lambda i: (i, 0)) for heads in (32, 32, 8, 8)]
    dma = pltpu.SemaphoreType.DMA
    group = target_group.reshape(1, ROWS)
    doc = document.reshape(1, ROWS)
    kv_shape = (KVH, 2, 2, NZ * HALF, HD)
    heads_shape = (HEADS, SLOTS, HD)
    piece_shape = (PIECES, NG, CAP, UNITS, HD)
    message_shape = (SETS, NG, 3, 16, HD)
    out_shape = [
        jax.ShapeDtypeStruct((ROWS, HEADS * HD), BF16),
        jax.ShapeDtypeStruct((ROWS, HEADS * HD), BF16),
        jax.ShapeDtypeStruct((ROWS, KVH * HD), BF16),
        jax.ShapeDtypeStruct((ROWS, KVH * HD), BF16),
    ]
    result = pl.pallas_call(
        whole_kernel,
        out_shape=out_shape,
        in_specs=[vmem] * 6,
        out_specs=[vmem] * 4,
        scratch_shapes=[
            pltpu.VMEM(kv_shape, BF16),
            pltpu.VMEM((NZ, 16, HD), BF16),
            pltpu.VMEM(heads_shape, BF16),
            pltpu.VMEM(heads_shape, BF16),
            pltpu.VMEM(heads_shape, BF16),
            pltpu.VMEM(heads_shape, BF16),
            pltpu.VMEM(kv_shape, BF16),
            pltpu.VMEM((KEYS, LANES), F32),
            pltpu.VMEM((KEYS, LANES), BF16),
            pltpu.VMEM((KEYS, LANES), BF16),
            pltpu.VMEM(message_shape, BF16),
            pltpu.VMEM(message_shape, BF16),
            pltpu.VMEM(piece_shape, BF16),
            pltpu.VMEM(piece_shape, BF16),
            pltpu.VMEM(message_shape, BF16),
            pltpu.VMEM(message_shape, BF16),
            pltpu.VMEM(piece_shape, BF16),
            pltpu.VMEM((KVH, 2, NZ - 1, 2, HALF, HD), BF16),
            dma((SETS,)), dma((SETS,)), dma((SETS,)),
            dma((PIECES,)), dma((PIECES,)), dma((PIECES,)),
            dma((SETS,)), dma((SETS,)), dma((SETS,)),
            dma((PIECES,)), dma((PIECES,)), dma((PIECES,)),
            dma((KVH, 2, NZ - 1)), dma((KVH, 2, NZ - 1)),
            dma((KVH, 2, NZ - 1)), dma((KVH, 2, NZ - 1)),
            dma((NZ - 1,)), dma((NZ - 1,)),
        ],
        compiler_params=pltpu.CompilerParams(
            collective_id=0, has_side_effects=True, vmem_limit_bytes=VMEM_LIMIT
        ),
        name="whole",
    )(query, key_states, value_states, out_grad, group, doc)
    return tuple(
        pl.pallas_call(
            copy_kernel,
            out_shape=out_shape,
            grid=(4,),
            in_specs=blocks,
            out_specs=blocks,
            name="place_outputs",
        )(*result)
    )


def solution(mesh):
    rows = P(("dp", "seq"), None)
    line = P(("dp", "seq"))
    return jax.shard_map(
        per_device,
        mesh=mesh,
        in_specs=(rows, rows, rows, rows, line, line),
        out_specs=(rows, rows, rows, rows),
        check_vma=False,
    )
```

```python
import math

import jax
import jax.numpy as jnp
from jax import lax
from jax.experimental import pallas as pl
from jax.experimental.pallas import tpu as pltpu
from jax.sharding import PartitionSpec as P

HD = 128
NX, NZ, NS = 4, 8, 8
NG = NX * NS
CAP = 5
SLOTS = NG * CAP
HALF = SLOTS // 2
KEYS = NZ * SLOTS
HEADS, KVH, RATIO = 32, 8, 4
UNITS = 16
PIECES = 4
ROWS = 128
BLK = 16
SET = KVH // 2
SETS = 2
WIDE = 8
LANES = RATIO * SLOTS
SPLIT = 256
INV_ROOT = 1.0 / math.sqrt(HD)
MESH = pl.DeviceIdType.MESH
BF16 = jnp.bfloat16
F32 = jnp.float32
VMEM_LIMIT = 56 * 1024 * 1024


def iota(shape, dim):
    return lax.broadcasted_iota(jnp.int32, shape, dim)


def dot(a, b):
    return lax.dot_general(a, b, (((1,), (0,)), ((), ())), preferred_element_type=F32)


def dot_nt(a, b):
    return lax.dot_general(a, b, (((1,), (1,)), ((), ())), preferred_element_type=F32)


def place():
    dp, seq = lax.axis_index("dp"), lax.axis_index("seq")
    return dp // NZ, lax.rem(dp, NZ), seq


def plane_device(x, z, seq, step):
    to = lax.rem(x * NS + seq + step, NG)
    return to, (lax.div(to, NS) * NZ + z, lax.rem(to, NS))


def slot_matrix(group_ref, width):
    across = jnp.broadcast_to(group_ref[...], (ROWS, ROWS)).astype(F32)
    down = across.T
    earlier = (across == down) & (iota((ROWS, ROWS), 0) < iota((ROWS, ROWS), 1))
    rank = jnp.sum(earlier.astype(F32), axis=0, keepdims=True)
    slot = across[:1] * width + rank
    return (iota((NG * width, ROWS), 0).astype(F32) == slot).astype(BF16)


def transposed(matrix):
    return matrix.astype(F32).T.astype(BF16)


def swap_tiles(swap, tiles):
    mixed = dot(swap, jnp.concatenate(tiles, axis=0)).astype(BF16)
    return [mixed[i * 16 : (i + 1) * 16] for i in range(mixed.shape[0] // 16)]


def greet(x, z, seq, ring):
    barrier = pltpu.get_barrier_semaphore()

    def signal(step, carry):
        _, device = plane_device(x, z, seq, step)
        pl.semaphore_signal(barrier, inc=1, device_id=device, device_id_type=MESH)
        return carry

    for device in ring:
        pl.semaphore_signal(barrier, inc=1, device_id=device, device_id_type=MESH)
    lax.fori_loop(1, NG, signal, 0)
    return barrier


def exchange_start(x, z, seq, send, recv, send_sem, recv_sem, own_sem):
    me = x * NS + seq

    def one(step, carry):
        to, device = plane_device(x, z, seq, step)
        pltpu.make_async_remote_copy(
            src_ref=send.at[to],
            dst_ref=recv.at[me],
            send_sem=send_sem,
            recv_sem=recv_sem,
            device_id=device,
            device_id_type=MESH,
        ).start()
        return carry

    lax.fori_loop(1, NG, one, 0)
    pltpu.make_async_copy(send.at[me], recv.at[me], own_sem).start()


def exchange_wait_recv(recv, recv_sem, own_sem):
    pltpu.make_async_copy(recv.at[pl.ds(0, NG - 1)], recv.at[pl.ds(0, NG - 1)], recv_sem).wait()
    pltpu.make_async_copy(recv.at[0], recv.at[0], own_sem).wait()


def exchange_wait_send(send, send_sem):
    pltpu.make_async_copy(send.at[pl.ds(0, NG - 1)], send.at[pl.ds(0, NG - 1)], send_sem).wait()


def token_tiles(ref, piece, block):
    return [ref[piece, t // CAP, t % CAP] for t in range(block * BLK, block * BLK + BLK)]


def put_tiles(ref, piece, block, tiles):
    for i, tile in enumerate(tiles):
        t = block * BLK + i
        ref[piece, t // CAP, t % CAP] = tile


def message_from_wide():
    out, src = iota((192, 256), 0), iota((192, 256), 1)
    group, row, unit = out // 48, lax.rem(out, 48) // 8, lax.rem(out, 8)
    return (src == unit * 32 + group * 8 + row).astype(BF16)


def units_from_message(block):
    out, src = iota((128, 192), 0), iota((128, 192), 1)
    slot = block * BLK + lax.rem(out, BLK) - first_message(block) * CAP
    return (src == (slot // CAP) * 48 + lax.rem(slot, CAP) * 8 + out // BLK).astype(BF16)


def first_message(block):
    return block * BLK // CAP


def message_from_units(four):
    out, src = iota((192, 256), 0), iota((192, 256), 1)
    row, unit = lax.rem(out, 48) // 8, lax.rem(out, 8)
    slot = four * 4 * CAP + (out // 48) * CAP + row - (four * 4 * CAP // BLK) * BLK
    return ((src == unit * 32 + slot) & (row < CAP)).astype(BF16)


def query_slots(rows):
    lane = iota((rows, LANES), 1)
    return (lane // (RATIO * HALF)) * HALF + lax.rem(lane, HALF)


def query_codes(meta):
    expand = (iota((HD, LANES), 0) == lax.rem(query_slots(HD), 20)).astype(BF16)
    own = iota((16, LANES), 0) == 8 + query_slots(16) // 20
    return jnp.sum(jnp.where(own, dot(meta, expand), 0.0), axis=0, keepdims=True)


def mask_block(meta_ref, bias, z, zk):
    tq = query_slots(1)
    code_q = query_codes(meta_ref[z])
    order_q = (tq // 40) * 320 + z * 40 + lax.rem(tq, 40)
    slot, lane = iota((SLOTS, HD), 0), iota((SLOTS, HD), 1)
    spread = (8 + iota((SLOTS, 16), 0) // 20 == iota((SLOTS, 16), 1)).astype(BF16)
    picked = jnp.where(lane == lax.rem(slot, 20), dot(spread, meta_ref[zk]), 0.0).astype(BF16)
    code_k = dot(picked, jnp.ones((HD, HD), BF16))
    order_k = (slot // 40) * 320 + zk * 40 + lax.rem(slot, 40)
    for half in range(2):
        rows = slice(half * HALF, (half + 1) * HALF)
        at_row = pl.multiple_of(half * NZ * HALF + zk * HALF, BLK)
        for at in range(0, LANES, HD):
            cols = slice(at, at + HD)
            ok = (
                (code_k[rows] == code_q[:, cols])
                & (code_k[rows] > 0.5)
                & (order_k[rows] <= order_q[:, cols])
            )
            bias[pl.ds(at_row, HALF), cols] = jnp.where(ok, 0.0, -1e30)


def attend_head(
    c, kv_ref, q_ref, g_ref, o_ref, dq_ref, dkv_ref, bias, p_ref, ds_ref, between
):
    log_scale = INV_ROOT * math.log2(math.e)

    def rows_of(ref):
        return jnp.concatenate(
            [
                ref[c * RATIO + h, half * HALF : (half + 1) * HALF, :]
                for half in range(2)
                for h in range(RATIO)
            ],
            axis=0,
        )

    q, g = rows_of(q_ref), rows_of(g_ref)
    k = kv_ref[c, 0].reshape(KEYS, HD)
    v = kv_ref[c, 1].reshape(KEYS, HD)
    kt, vt = k.T, v.T
    blocks = ((0, SPLIT, KEYS // 2), (SPLIT, 2 * SPLIT, KEYS), (2 * SPLIT, LANES, KEYS))
    outs, dqs = [], []

    def products(i):
        lo, hi, n = blocks[i]
        return dot_nt(k[:n], q[lo:hi]), dot_nt(v[:n], g[lo:hi])

    def softmax(i, s, dp):
        lo, hi, n = blocks[i]
        s = s * log_scale + bias[:n, lo:hi]
        e = jnp.exp2(s - jnp.max(s, axis=0, keepdims=True))
        scale = 1.0 / jnp.sum(e, axis=0, keepdims=True)
        delta = jnp.sum(e * dp, axis=0, keepdims=True) * scale
        p = e * scale
        low, ds = p.astype(BF16), (p * (dp - delta)).astype(BF16)
        p_ref[:n, lo:hi] = low
        ds_ref[:n, lo:hi] = ds
        return low, ds

    def results(i, low, ds):
        n = blocks[i][2]
        outs.append(dot(vt[:, :n], low).astype(BF16).T)
        dqs.append((dot(kt[:, :n], ds) * INV_ROOT).astype(BF16).T)

    first, second = products(0), products(1)
    done = softmax(0, *first)
    between(0)
    third = products(2)
    after = softmax(1, *second)
    results(0, *done)
    between(1)
    done = softmax(2, *third)
    results(1, *after)
    between(2)
    results(2, *done)
    n = KEYS // 2
    for half, lo in ((0, 0), (1, SPLIT)):
        rows = slice(half * n, (half + 1) * n)
        dkv_ref[c, 0, half] = (dot(ds_ref[rows, lo:], q[lo:]) * INV_ROOT).astype(BF16)
        dkv_ref[c, 1, half] = dot(p_ref[rows, lo:], g[lo:]).astype(BF16)
        if half == 0:
            between(3)
    out, dq = jnp.concatenate(outs, axis=0), jnp.concatenate(dqs, axis=0)
    for half in range(2):
        for h in range(RATIO):
            rows = slice((half * RATIO + h) * HALF, (half * RATIO + h + 1) * HALF)
            o_ref[c * RATIO + h, half * HALF : (half + 1) * HALF, :] = out[rows]
            dq_ref[c * RATIO + h, half * HALF : (half + 1) * HALF, :] = dq[rows]


def whole_kernel(
    q_ref, k_ref, v_ref, g_ref, group_ref, doc_ref,
    out_ref, qg_ref, kg_ref, vg_ref,
    kv_ref, meta_ref, qu_ref, gu_ref, ou_ref, dqu_ref, dkv_ref,
    bias, p_ref, ds_ref,
    send0, recv0, send, recv, dkv_send, back0, back, land,
    kv_s, kv_r, kv_o, row_s, row_r, row_o, dkv_s, dkv_r, dkv_o, res_s, res_r, res_o,
    ring_s, ring_r, sum_s, sum_r, meta_s, meta_r,
):
    x, z, seq = place()
    me = x * NS + seq
    right = (x * NZ + lax.rem(z + 1, NZ), seq)
    left = (x * NZ + lax.rem(z + NZ - 1, NZ), seq)
    barrier = greet(x, z, seq, (left, right))

    pick = slot_matrix(group_ref, CAP)
    pick_wide = slot_matrix(group_ref, WIDE)
    row, col = iota((256, 256), 0), iota((256, 256), 1)
    swap = (col == lax.rem(row, 16) * 16 + row // 16).astype(BF16)

    def rows_pack(piece):
        cols = slice(piece * 1024, (piece + 1) * 1024)
        packed = [dot(pick, part[:, cols]).astype(BF16) for part in (q_ref, g_ref)]
        for block in range(SLOTS // BLK):
            rows = slice(block * BLK, (block + 1) * BLK)
            tiles = [part[rows, at * HD : (at + 1) * HD] for part in packed for at in range(8)]
            put_tiles(send, piece, block, swap_tiles(swap, tiles))

    def rows_start(piece):
        exchange_start(
            x, z, seq, send.at[piece], recv.at[piece],
            row_s.at[piece], row_r.at[piece], row_o.at[piece],
        )

    def rows_unpack(piece):
        exchange_wait_recv(recv.at[piece], row_r.at[piece], row_o.at[piece])
        for block in range(SLOTS // BLK):
            tiles = swap_tiles(swap, token_tiles(recv, piece, block))
            rows = slice(block * BLK, (block + 1) * BLK)
            for unit in range(8):
                qu_ref[piece * 8 + unit, rows, :] = tiles[unit]
                gu_ref[piece * 8 + unit, rows, :] = tiles[8 + unit]

    def results_start(piece):
        exchange_wait_send(send.at[piece], row_s.at[piece])
        for block in range(SLOTS // BLK):
            rows = slice(block * BLK, (block + 1) * BLK)
            tiles = [ou_ref[piece * 8 + unit, rows, :] for unit in range(8)]
            tiles += [dqu_ref[piece * 8 + unit, rows, :] for unit in range(8)]
            put_tiles(send, piece, block, swap_tiles(swap, tiles))
        exchange_start(
            x, z, seq, send.at[piece], back.at[piece],
            res_s.at[piece], res_r.at[piece], res_o.at[piece],
        )

    def results_unpack(piece):
        exchange_wait_recv(back.at[piece], res_r.at[piece], res_o.at[piece])
        pick_t = transposed(pick)
        parts = [[] for _ in range(UNITS)]
        for block in range(SLOTS // BLK):
            tiles = swap_tiles(swap, token_tiles(back, piece, block))
            for unit in range(UNITS):
                parts[unit].append(tiles[unit])
        for unit in range(UNITS):
            rows = jnp.concatenate(parts[unit], axis=0)
            at = (piece * 8 + unit % 8) * HD
            (out_ref, qg_ref)[unit // 8][:, at : at + HD] = dot(pick_t, rows).astype(BF16)

    def keys_pack(part, extra, mix):
        packed = []
        for unit in range(8):
            at = (part * SET + unit // 2) * HD
            rows = dot(pick_wide, (k_ref, v_ref)[unit % 2][:, at : at + HD])
            if extra is not None:
                rows = rows + jnp.where(me // 4 == unit, extra, 0.0)
            packed.append(rows.astype(BF16))
        for four in range(NG // 4):
            rows = slice(four * 32, (four + 1) * 32)
            tiles = swap_tiles(mix, [part_rows[rows] for part_rows in packed])
            for i, tile in enumerate(tiles):
                send0[part, four * 4 + i // 3, i % 3] = tile

    def keys_start(part):
        exchange_start(
            x, z, seq, send0.at[part], recv0.at[part],
            kv_s.at[part], kv_r.at[part], kv_o.at[part],
        )

    def keys_unpack(part):
        exchange_wait_recv(recv0.at[part], kv_r.at[part], kv_o.at[part])
        here = pl.multiple_of(z * HALF, BLK)
        for block in range(SLOTS // BLK):
            first = first_message(block)
            tiles = [recv0[part, first + i // 3, i % 3] for i in range(12)]
            tiles = swap_tiles(units_from_message(block), tiles)
            half, at = block // 5, (block % 5) * BLK
            for unit in range(8):
                kv_ref[part * SET + unit // 2, unit % 2, half, pl.ds(here + at, BLK), :] = tiles[
                    unit
                ]

    def terms_start(part):
        for four in range(NG // 4):
            lo = four * 4 * CAP // BLK * BLK
            tiles = []
            for unit in range(8):
                for at in (lo, lo + BLK):
                    half, in_half = at // HALF, at % HALF
                    tiles.append(
                        land[part * SET + unit // 2, unit % 2, NZ - 2, half, in_half : in_half + BLK, :]
                    )
            tiles = swap_tiles(message_from_units(four), tiles)
            for i, tile in enumerate(tiles):
                dkv_send[part, four * 4 + i // 3, i % 3] = tile
        exchange_start(
            x, z, seq, dkv_send.at[part], back0.at[part],
            dkv_s.at[part], dkv_r.at[part], dkv_o.at[part],
        )

    def terms_unpack(part):
        exchange_wait_recv(back0.at[part], dkv_r.at[part], dkv_o.at[part])
        pick_t = transposed(pick_wide)
        mix = transposed(message_from_wide())
        parts = [[] for _ in range(8)]
        for four in range(NG // 4):
            tiles = [back0[part, four * 4 + i // 3, i % 3] for i in range(12)]
            tiles = swap_tiles(mix, tiles)
            for unit in range(8):
                parts[unit] += tiles[2 * unit : 2 * unit + 2]
        for unit in range(8):
            rows = jnp.concatenate(parts[unit], axis=0)
            at = (part * SET + unit // 2) * HD
            (kg_ref, vg_ref)[unit % 2][:, at : at + HD] = dot(pick_t, rows).astype(BF16)

    def plane(index):
        return pl.ds(pl.multiple_of(index * HALF, BLK), HALF)

    def way(head):
        return 1 + lax.rem(head, 2) * (NZ - 2)

    def neighbour(head):
        return (x * NZ + lax.rem(z + way(head), NZ), seq)

    def gather_copy(head, which, step):
        owner = lax.rem(z + (NZ - way(head)) * step, NZ)
        block = kv_ref.at[head, which, :, plane(owner), :]
        return pltpu.make_async_remote_copy(
            src_ref=block,
            dst_ref=block,
            send_sem=ring_s.at[head, which, step],
            recv_sem=ring_r.at[head, which, step],
            device_id=neighbour(head),
            device_id_type=MESH,
        )

    def meta_copy(step):
        owner = lax.rem(z - step + NZ, NZ)
        return pltpu.make_async_remote_copy(
            src_ref=meta_ref.at[owner],
            dst_ref=meta_ref.at[owner],
            send_sem=meta_s.at[step],
            recv_sem=meta_r.at[step],
            device_id=right,
            device_id_type=MESH,
        )

    def terms_for(head, step):
        return plane(lax.rem(z + (NZ - way(head)) * (step + 1), NZ))

    def sum_copy(head, which, step, src):
        return pltpu.make_async_remote_copy(
            src_ref=src,
            dst_ref=land.at[head, which, step],
            send_sem=sum_s.at[head, which, step],
            recv_sem=sum_r.at[head, which, step],
            device_id=neighbour(head),
            device_id_type=MESH,
        )

    def sum_first(head):
        for which in range(2):
            src = dkv_ref.at[head, which, :, terms_for(head, 0), :]
            sum_copy(head, which, 0, src).start()

    def sum_next(head, which, step):
        slot = land.at[head, which, step - 1]
        sum_copy(head, which, step - 1, slot).wait_recv()
        own = dkv_ref[head, which, :, terms_for(head, step), :]
        slot[...] = (own.astype(F32) + slot[...].astype(F32)).astype(BF16)

        def send_on():
            sum_copy(head, which, step, slot).start()

        if isinstance(step, int):
            if step < NZ - 1:
                send_on()
        else:
            pl.when(step < NZ - 1)(send_on)

    code = dot_nt(pick_wide, jnp.broadcast_to(doc_ref[...] + 1, (HD, ROWS)).astype(BF16))
    slot, lane = iota((256, HD), 0), iota((256, HD), 1)
    code = jnp.where(lane == lax.rem(me, 4) * CAP + lax.rem(slot, WIDE), code, 0.0).astype(BF16)
    sel = ((row // WIDE == col // WIDE) & (lax.rem(row, WIDE) == CAP)).astype(BF16)
    mix = message_from_wide()
    keys_pack(0, dot(sel, code), mix)
    pl.semaphore_wait(barrier, NG + 1)
    keys_start(0)
    keys_pack(1, None, mix)
    for piece in (0, 1):
        rows_pack(piece)

    keys_unpack(0)
    total = recv0[0, 0, 2]
    for s in range(1, NG):
        total = total + recv0[0, s, 2]
    meta_ref[z] = total

    heads = (0, 1, 2, 3)
    for step in range(NZ - 1):
        for which in range(2):
            for head in heads:
                if step > 0:
                    gather_copy(head, which, step - 1).wait_recv()
                gather_copy(head, which, step).start()
        if step > 0:
            meta_copy(step - 1).wait_recv()
        meta_copy(step).start()
        if step == 0:
            keys_start(1)
        if step < PIECES:
            if step >= 2:
                rows_pack(step)
            rows_start(step)
        mask_block(meta_ref, bias, z, lax.rem(z - step + NZ, NZ))
        if step == 4:
            keys_unpack(1)
        if step >= 5:
            rows_unpack(step - 5)
    for which in range(2):
        for head in heads:
            gather_copy(SET + head, which, 0).start()
    meta_copy(NZ - 2).wait_recv()
    mask_block(meta_ref, bias, z, lax.rem(z + 1, NZ))
    for which in range(2):
        for head in heads:
            gather_copy(head, which, NZ - 2).wait_recv()

    refs = (kv_ref, qu_ref, gu_ref, ou_ref, dqu_ref, dkv_ref, bias, p_ref, ds_ref)

    def hop_of(event):
        pair = lax.rem(event, 2) * 2
        return 1 + event // 4, lax.rem(event // 2, 2), (pair, pair + 1)

    def first_heads(i, carry):
        def between(at):
            step, which, pair = hop_of(7 * i + at)
            for head in pair:
                gather_copy(SET + head, which, step - 1).wait_recv()

                @pl.when(step < NZ - 1)
                def _():
                    gather_copy(SET + head, which, step).start()

        attend_head(i, *refs, between)
        sum_first(i)
        between(4)

        @pl.when(i >= 2)
        def _():
            rows_unpack(i)

        between(5)

        @pl.when(lax.rem(i, 2) == 1)
        def _():
            results_start(i // 2)

        between(6)
        return carry

    lax.fori_loop(0, SET, first_heads, 0)

    def other_heads(i, carry):
        def between(at):
            step, which, pair = hop_of(7 * i + at)
            for head in pair:
                sum_next(head, which, step)

        attend_head(i + SET, *refs, between)
        sum_first(i + SET)
        between(4)
        between(5)

        @pl.when(lax.rem(i, 2) == 1)
        def _():
            results_start(2 + i // 2)

        between(6)
        return carry

    lax.fori_loop(0, SET, other_heads, 0)
    for step in range(1, NZ):
        for which in range(2):
            for head in heads:
                sum_next(SET + head, which, step)
        if step == 1:
            terms_start(0)
        if step in (3, 4):
            results_unpack(step - 3)
        if step == 6:
            terms_unpack(0)
    terms_start(1)
    for piece in (2, 3):
        results_unpack(piece)

    def ring_sent(step, carry):
        for which in range(2):
            for head in range(KVH):
                gather_copy(head, which, step).wait_send()
                sum_copy(head, which, step, land.at[head, which, step]).wait_send()
        meta_copy(step).wait_send()
        return carry

    lax.fori_loop(0, NZ - 1, ring_sent, 0)
    exchange_wait_send(dkv_send.at[0], dkv_s.at[0])
    for part in range(SETS):
        exchange_wait_send(send0.at[part], kv_s.at[part])
    for piece in range(PIECES):
        exchange_wait_send(send.at[piece], res_s.at[piece])
    terms_unpack(1)
    exchange_wait_send(dkv_send.at[1], dkv_s.at[1])


def copy_kernel(*refs):
    srcs, dsts, held, into, out_of = refs[:4], refs[4:8], refs[8:12], refs[12], refs[13]
    loads, stores = [], []
    for src, dst, buf in zip(srcs, dsts, held):
        for part in range(4):
            rows, n = pl.ds(part * 32, 32), len(loads)
            loads.append(pltpu.make_async_copy(src.at[rows], buf.at[rows], into.at[n]))
            stores.append(pltpu.make_async_copy(buf.at[rows], dst.at[rows], out_of.at[n]))
    for load in loads:
        load.start()
    for load, store in zip(loads, stores):
        load.wait()
        store.start()
    for store in stores:
        store.wait()


def per_device(query, key_states, value_states, out_grad, target_group, document):
    vmem = pl.BlockSpec(memory_space=pltpu.VMEM)
    anywhere = pl.BlockSpec(memory_space=pl.ANY)
    dma = pltpu.SemaphoreType.DMA
    group = target_group.reshape(1, ROWS)
    doc = document.reshape(1, ROWS)
    kv_shape = (KVH, 2, 2, NZ * HALF, HD)
    heads_shape = (HEADS, SLOTS, HD)
    piece_shape = (PIECES, NG, CAP, UNITS, HD)
    message_shape = (SETS, NG, 3, 16, HD)
    out_shape = [
        jax.ShapeDtypeStruct((ROWS, HEADS * HD), BF16),
        jax.ShapeDtypeStruct((ROWS, HEADS * HD), BF16),
        jax.ShapeDtypeStruct((ROWS, KVH * HD), BF16),
        jax.ShapeDtypeStruct((ROWS, KVH * HD), BF16),
    ]
    result = pl.pallas_call(
        whole_kernel,
        out_shape=out_shape,
        in_specs=[vmem] * 6,
        out_specs=[vmem] * 4,
        scratch_shapes=[
            pltpu.VMEM(kv_shape, BF16),
            pltpu.VMEM((NZ, 16, HD), BF16),
            pltpu.VMEM(heads_shape, BF16),
            pltpu.VMEM(heads_shape, BF16),
            pltpu.VMEM(heads_shape, BF16),
            pltpu.VMEM(heads_shape, BF16),
            pltpu.VMEM(kv_shape, BF16),
            pltpu.VMEM((KEYS, LANES), F32),
            pltpu.VMEM((KEYS, LANES), BF16),
            pltpu.VMEM((KEYS, LANES), BF16),
            pltpu.VMEM(message_shape, BF16),
            pltpu.VMEM(message_shape, BF16),
            pltpu.VMEM(piece_shape, BF16),
            pltpu.VMEM(piece_shape, BF16),
            pltpu.VMEM(message_shape, BF16),
            pltpu.VMEM(message_shape, BF16),
            pltpu.VMEM(piece_shape, BF16),
            pltpu.VMEM((KVH, 2, NZ - 1, 2, HALF, HD), BF16),
            dma((SETS,)), dma((SETS,)), dma((SETS,)),
            dma((PIECES,)), dma((PIECES,)), dma((PIECES,)),
            dma((SETS,)), dma((SETS,)), dma((SETS,)),
            dma((PIECES,)), dma((PIECES,)), dma((PIECES,)),
            dma((KVH, 2, NZ - 1)), dma((KVH, 2, NZ - 1)),
            dma((KVH, 2, NZ - 1)), dma((KVH, 2, NZ - 1)),
            dma((NZ - 1,)), dma((NZ - 1,)),
        ],
        compiler_params=pltpu.CompilerParams(
            collective_id=0, has_side_effects=True, vmem_limit_bytes=VMEM_LIMIT
        ),
        name="whole",
    )(query, key_states, value_states, out_grad, group, doc)
    return tuple(
        pl.pallas_call(
            copy_kernel,
            out_shape=out_shape,
            in_specs=[anywhere] * 4,
            out_specs=[anywhere] * 4,
            scratch_shapes=[pltpu.VMEM(shape.shape, BF16) for shape in out_shape]
            + [dma((16,)), dma((16,))],
            name="place_outputs",
        )(*result)
    )


def solution(mesh):
    rows = P(("dp", "seq"), None)
    line = P(("dp", "seq"))
    return jax.shard_map(
        per_device,
        mesh=mesh,
        in_specs=(rows, rows, rows, rows, line, line),
        out_specs=(rows, rows, rows, rows),
        check_vma=False,
    )
```

```python
import math

import jax
import jax.numpy as jnp
from jax import lax
from jax.experimental import pallas as pl
from jax.experimental.pallas import tpu as pltpu
from jax.sharding import PartitionSpec as P

HD = 128
NX, NZ, NS = 4, 8, 8
NG = NX * NS
CAP = 5
SLOTS = NG * CAP
HALF = SLOTS // 2
KEYS = NZ * SLOTS
HEADS, KVH, RATIO = 32, 8, 4
UNITS = 16
PIECES = 4
ROWS = 128
BLK = 16
SET = KVH // 2
SETS = 2
WIDE = 8
LANES = RATIO * SLOTS
SPLIT = 256
INV_ROOT = 1.0 / math.sqrt(HD)
MESH = pl.DeviceIdType.MESH
BF16 = jnp.bfloat16
F32 = jnp.float32
VMEM_LIMIT = 56 * 1024 * 1024


def iota(shape, dim):
    return lax.broadcasted_iota(jnp.int32, shape, dim)


def dot(a, b):
    return lax.dot_general(a, b, (((1,), (0,)), ((), ())), preferred_element_type=F32)


def dot_nt(a, b):
    return lax.dot_general(a, b, (((1,), (1,)), ((), ())), preferred_element_type=F32)


def place():
    dp, seq = lax.axis_index("dp"), lax.axis_index("seq")
    return dp // NZ, lax.rem(dp, NZ), seq


def plane_device(x, z, seq, step):
    to = lax.rem(x * NS + seq + step, NG)
    return to, (lax.div(to, NS) * NZ + z, lax.rem(to, NS))


def slot_matrix(group_ref, width):
    across = jnp.broadcast_to(group_ref[...], (ROWS, ROWS)).astype(F32)
    down = across.T
    earlier = (across == down) & (iota((ROWS, ROWS), 0) < iota((ROWS, ROWS), 1))
    rank = jnp.sum(earlier.astype(F32), axis=0, keepdims=True)
    slot = across[:1] * width + rank
    return (iota((NG * width, ROWS), 0).astype(F32) == slot).astype(BF16)


def transposed(matrix):
    return matrix.astype(F32).T.astype(BF16)


def swap_tiles(swap, tiles):
    mixed = dot(swap, jnp.concatenate(tiles, axis=0)).astype(BF16)
    return [mixed[i * 16 : (i + 1) * 16] for i in range(mixed.shape[0] // 16)]


def greet(x, z, seq, ring):
    barrier = pltpu.get_barrier_semaphore()

    def signal(step, carry):
        _, device = plane_device(x, z, seq, step)
        pl.semaphore_signal(barrier, inc=1, device_id=device, device_id_type=MESH)
        return carry

    for device in ring:
        pl.semaphore_signal(barrier, inc=1, device_id=device, device_id_type=MESH)
    lax.fori_loop(1, NG, signal, 0)
    return barrier


def exchange_start(x, z, seq, send, recv, send_sem, recv_sem, own_sem):
    me = x * NS + seq

    def one(step, carry):
        to, device = plane_device(x, z, seq, step)
        pltpu.make_async_remote_copy(
            src_ref=send.at[to],
            dst_ref=recv.at[me],
            send_sem=send_sem,
            recv_sem=recv_sem,
            device_id=device,
            device_id_type=MESH,
        ).start()
        return carry

    lax.fori_loop(1, NG, one, 0)
    pltpu.make_async_copy(send.at[me], recv.at[me], own_sem).start()


def exchange_wait_recv(recv, recv_sem, own_sem):
    pltpu.make_async_copy(recv.at[pl.ds(0, NG - 1)], recv.at[pl.ds(0, NG - 1)], recv_sem).wait()
    pltpu.make_async_copy(recv.at[0], recv.at[0], own_sem).wait()


def exchange_wait_send(send, send_sem):
    pltpu.make_async_copy(send.at[pl.ds(0, NG - 1)], send.at[pl.ds(0, NG - 1)], send_sem).wait()


def token_tiles(ref, piece, block):
    return [ref[piece, t // CAP, t % CAP] for t in range(block * BLK, block * BLK + BLK)]


def put_tiles(ref, piece, block, tiles):
    for i, tile in enumerate(tiles):
        t = block * BLK + i
        ref[piece, t // CAP, t % CAP] = tile


def message_from_wide():
    out, src = iota((192, 256), 0), iota((192, 256), 1)
    group, row, unit = out // 48, lax.rem(out, 48) // 8, lax.rem(out, 8)
    return (src == unit * 32 + group * 8 + row).astype(BF16)


def units_from_message(block):
    out, src = iota((128, 192), 0), iota((128, 192), 1)
    slot = block * BLK + lax.rem(out, BLK) - first_message(block) * CAP
    return (src == (slot // CAP) * 48 + lax.rem(slot, CAP) * 8 + out // BLK).astype(BF16)


def first_message(block):
    return block * BLK // CAP


def message_from_units(four):
    out, src = iota((192, 256), 0), iota((192, 256), 1)
    row, unit = lax.rem(out, 48) // 8, lax.rem(out, 8)
    slot = four * 4 * CAP + (out // 48) * CAP + row - (four * 4 * CAP // BLK) * BLK
    return ((src == unit * 32 + slot) & (row < CAP)).astype(BF16)


def query_slots(rows):
    lane = iota((rows, LANES), 1)
    return (lane // (RATIO * HALF)) * HALF + lax.rem(lane, HALF)


def query_codes(meta):
    expand = (iota((HD, LANES), 0) == lax.rem(query_slots(HD), 20)).astype(BF16)
    own = iota((16, LANES), 0) == 8 + query_slots(16) // 20
    return jnp.sum(jnp.where(own, dot(meta, expand), 0.0), axis=0, keepdims=True)


def mask_block(meta_ref, bias, z, zk):
    tq = query_slots(1)
    code_q = query_codes(meta_ref[z])
    order_q = (tq // 40) * 320 + z * 40 + lax.rem(tq, 40)
    slot, lane = iota((SLOTS, HD), 0), iota((SLOTS, HD), 1)
    spread = (8 + iota((SLOTS, 16), 0) // 20 == iota((SLOTS, 16), 1)).astype(BF16)
    picked = jnp.where(lane == lax.rem(slot, 20), dot(spread, meta_ref[zk]), 0.0).astype(BF16)
    code_k = dot(picked, jnp.ones((HD, HD), BF16))
    order_k = (slot // 40) * 320 + zk * 40 + lax.rem(slot, 40)
    for half in range(2):
        rows = slice(half * HALF, (half + 1) * HALF)
        at_row = pl.multiple_of(half * NZ * HALF + zk * HALF, BLK)
        for at in range(0, LANES, HD):
            cols = slice(at, at + HD)
            ok = (
                (code_k[rows] == code_q[:, cols])
                & (code_k[rows] > 0.5)
                & (order_k[rows] <= order_q[:, cols])
            )
            bias[pl.ds(at_row, HALF), cols] = jnp.where(ok, 0.0, -1e30)


def attend_head(
    c, kv_ref, q_ref, g_ref, o_ref, dq_ref, dkv_ref, bias, p_ref, ds_ref, between
):
    log_scale = INV_ROOT * math.log2(math.e)

    def rows_of(ref):
        return jnp.concatenate(
            [
                ref[c * RATIO + h, half * HALF : (half + 1) * HALF, :]
                for half in range(2)
                for h in range(RATIO)
            ],
            axis=0,
        )

    q, g = rows_of(q_ref), rows_of(g_ref)
    k = kv_ref[c, 0].reshape(KEYS, HD)
    v = kv_ref[c, 1].reshape(KEYS, HD)
    kt, vt = k.T, v.T
    blocks = ((0, SPLIT, KEYS // 2), (SPLIT, 2 * SPLIT, KEYS), (2 * SPLIT, LANES, KEYS))
    outs, dqs = [], []

    def products(i):
        lo, hi, n = blocks[i]
        return dot_nt(k[:n], q[lo:hi]), dot_nt(v[:n], g[lo:hi])

    def softmax(i, s, dp):
        lo, hi, n = blocks[i]
        s = s * log_scale + bias[:n, lo:hi]
        e = jnp.exp2(s - jnp.max(s, axis=0, keepdims=True))
        scale = 1.0 / jnp.sum(e, axis=0, keepdims=True)
        delta = jnp.sum(e * dp, axis=0, keepdims=True) * scale
        p = e * scale
        low, ds = p.astype(BF16), (p * (dp - delta)).astype(BF16)
        p_ref[:n, lo:hi] = low
        ds_ref[:n, lo:hi] = ds
        return low, ds

    def results(i, low, ds):
        n = blocks[i][2]
        outs.append(dot(vt[:, :n], low).astype(BF16).T)
        dqs.append((dot(kt[:, :n], ds) * INV_ROOT).astype(BF16).T)

    first, second = products(0), products(1)
    done = softmax(0, *first)
    between(0)
    third = products(2)
    after = softmax(1, *second)
    results(0, *done)
    between(1)
    done = softmax(2, *third)
    results(1, *after)
    between(2)
    results(2, *done)
    n = KEYS // 2
    for half, lo in ((0, 0), (1, SPLIT)):
        rows = slice(half * n, (half + 1) * n)
        dkv_ref[c, 0, half] = (dot(ds_ref[rows, lo:], q[lo:]) * INV_ROOT).astype(BF16)
        dkv_ref[c, 1, half] = dot(p_ref[rows, lo:], g[lo:]).astype(BF16)
        if half == 0:
            between(3)
    out, dq = jnp.concatenate(outs, axis=0), jnp.concatenate(dqs, axis=0)
    for half in range(2):
        for h in range(RATIO):
            rows = slice((half * RATIO + h) * HALF, (half * RATIO + h + 1) * HALF)
            o_ref[c * RATIO + h, half * HALF : (half + 1) * HALF, :] = out[rows]
            dq_ref[c * RATIO + h, half * HALF : (half + 1) * HALF, :] = dq[rows]


def whole_kernel(
    q_in, k_ref, v_ref, g_in, group_ref, doc_ref,
    out_hbm, qg_hbm, kg_ref, vg_ref,
    q_ref, g_ref, out_ref, qg_ref, load_sem, store_sem,
    kv_ref, meta_ref, qu_ref, gu_ref, ou_ref, dqu_ref, dkv_ref,
    bias, p_ref, ds_ref,
    send0, recv0, send, recv, dkv_send, back0, back, land,
    kv_s, kv_r, kv_o, row_s, row_r, row_o, dkv_s, dkv_r, dkv_o, res_s, res_r, res_o,
    ring_s, ring_r, sum_s, sum_r, meta_s, meta_r,
):
    x, z, seq = place()
    me = x * NS + seq
    right = (x * NZ + lax.rem(z + 1, NZ), seq)
    left = (x * NZ + lax.rem(z + NZ - 1, NZ), seq)
    loads = [
        pltpu.make_async_copy(src, dst, load_sem.at[i])
        for i, (src, dst) in enumerate(((q_in, q_ref), (g_in, g_ref)))
    ]
    stores = [
        pltpu.make_async_copy(src, dst, store_sem.at[i])
        for i, (src, dst) in enumerate(((out_ref, out_hbm), (qg_ref, qg_hbm)))
    ]
    barrier = greet(x, z, seq, (left, right))
    for load in loads:
        load.start()

    pick = slot_matrix(group_ref, CAP)
    pick_wide = slot_matrix(group_ref, WIDE)
    row, col = iota((256, 256), 0), iota((256, 256), 1)
    swap = (col == lax.rem(row, 16) * 16 + row // 16).astype(BF16)

    def rows_pack(piece):
        cols = slice(piece * 1024, (piece + 1) * 1024)
        packed = [dot(pick, part[:, cols]).astype(BF16) for part in (q_ref, g_ref)]
        for block in range(SLOTS // BLK):
            rows = slice(block * BLK, (block + 1) * BLK)
            tiles = [part[rows, at * HD : (at + 1) * HD] for part in packed for at in range(8)]
            put_tiles(send, piece, block, swap_tiles(swap, tiles))

    def rows_start(piece):
        exchange_start(
            x, z, seq, send.at[piece], recv.at[piece],
            row_s.at[piece], row_r.at[piece], row_o.at[piece],
        )

    def rows_unpack(piece):
        exchange_wait_recv(recv.at[piece], row_r.at[piece], row_o.at[piece])
        for block in range(SLOTS // BLK):
            tiles = swap_tiles(swap, token_tiles(recv, piece, block))
            rows = slice(block * BLK, (block + 1) * BLK)
            for unit in range(8):
                qu_ref[piece * 8 + unit, rows, :] = tiles[unit]
                gu_ref[piece * 8 + unit, rows, :] = tiles[8 + unit]

    def results_start(piece):
        exchange_wait_send(send.at[piece], row_s.at[piece])
        for block in range(SLOTS // BLK):
            rows = slice(block * BLK, (block + 1) * BLK)
            tiles = [ou_ref[piece * 8 + unit, rows, :] for unit in range(8)]
            tiles += [dqu_ref[piece * 8 + unit, rows, :] for unit in range(8)]
            put_tiles(send, piece, block, swap_tiles(swap, tiles))
        exchange_start(
            x, z, seq, send.at[piece], back.at[piece],
            res_s.at[piece], res_r.at[piece], res_o.at[piece],
        )

    def results_unpack(piece):
        exchange_wait_recv(back.at[piece], res_r.at[piece], res_o.at[piece])
        pick_t = transposed(pick)
        parts = [[] for _ in range(UNITS)]
        for block in range(SLOTS // BLK):
            tiles = swap_tiles(swap, token_tiles(back, piece, block))
            for unit in range(UNITS):
                parts[unit].append(tiles[unit])
        for unit in range(UNITS):
            rows = jnp.concatenate(parts[unit], axis=0)
            at = (piece * 8 + unit % 8) * HD
            (out_ref, qg_ref)[unit // 8][:, at : at + HD] = dot(pick_t, rows).astype(BF16)

    def keys_pack(part, extra, mix):
        packed = []
        for unit in range(8):
            at = (part * SET + unit // 2) * HD
            rows = dot(pick_wide, (k_ref, v_ref)[unit % 2][:, at : at + HD])
            if extra is not None:
                rows = rows + jnp.where(me // 4 == unit, extra, 0.0)
            packed.append(rows.astype(BF16))
        for four in range(NG // 4):
            rows = slice(four * 32, (four + 1) * 32)
            tiles = swap_tiles(mix, [part_rows[rows] for part_rows in packed])
            for i, tile in enumerate(tiles):
                send0[part, four * 4 + i // 3, i % 3] = tile

    def keys_start(part):
        exchange_start(
            x, z, seq, send0.at[part], recv0.at[part],
            kv_s.at[part], kv_r.at[part], kv_o.at[part],
        )

    def keys_unpack(part):
        exchange_wait_recv(recv0.at[part], kv_r.at[part], kv_o.at[part])
        here = pl.multiple_of(z * HALF, BLK)
        for block in range(SLOTS // BLK):
            first = first_message(block)
            tiles = [recv0[part, first + i // 3, i % 3] for i in range(12)]
            tiles = swap_tiles(units_from_message(block), tiles)
            half, at = block // 5, (block % 5) * BLK
            for unit in range(8):
                kv_ref[part * SET + unit // 2, unit % 2, half, pl.ds(here + at, BLK), :] = tiles[
                    unit
                ]

    def terms_start(part):
        for four in range(NG // 4):
            lo = four * 4 * CAP // BLK * BLK
            tiles = []
            for unit in range(8):
                for at in (lo, lo + BLK):
                    half, in_half = at // HALF, at % HALF
                    tiles.append(
                        land[part * SET + unit // 2, unit % 2, NZ - 2, half, in_half : in_half + BLK, :]
                    )
            tiles = swap_tiles(message_from_units(four), tiles)
            for i, tile in enumerate(tiles):
                dkv_send[part, four * 4 + i // 3, i % 3] = tile
        exchange_start(
            x, z, seq, dkv_send.at[part], back0.at[part],
            dkv_s.at[part], dkv_r.at[part], dkv_o.at[part],
        )

    def terms_unpack(part):
        exchange_wait_recv(back0.at[part], dkv_r.at[part], dkv_o.at[part])
        pick_t = transposed(pick_wide)
        mix = transposed(message_from_wide())
        parts = [[] for _ in range(8)]
        for four in range(NG // 4):
            tiles = [back0[part, four * 4 + i // 3, i % 3] for i in range(12)]
            tiles = swap_tiles(mix, tiles)
            for unit in range(8):
                parts[unit] += tiles[2 * unit : 2 * unit + 2]
        for unit in range(8):
            rows = jnp.concatenate(parts[unit], axis=0)
            at = (part * SET + unit // 2) * HD
            (kg_ref, vg_ref)[unit % 2][:, at : at + HD] = dot(pick_t, rows).astype(BF16)

    def plane(index):
        return pl.ds(pl.multiple_of(index * HALF, BLK), HALF)

    def way(head):
        return 1 + lax.rem(head, 2) * (NZ - 2)

    def neighbour(head):
        return (x * NZ + lax.rem(z + way(head), NZ), seq)

    def gather_copy(head, which, step):
        owner = lax.rem(z + (NZ - way(head)) * step, NZ)
        block = kv_ref.at[head, which, :, plane(owner), :]
        return pltpu.make_async_remote_copy(
            src_ref=block,
            dst_ref=block,
            send_sem=ring_s.at[head, which, step],
            recv_sem=ring_r.at[head, which, step],
            device_id=neighbour(head),
            device_id_type=MESH,
        )

    def meta_copy(step):
        owner = lax.rem(z - step + NZ, NZ)
        return pltpu.make_async_remote_copy(
            src_ref=meta_ref.at[owner],
            dst_ref=meta_ref.at[owner],
            send_sem=meta_s.at[step],
            recv_sem=meta_r.at[step],
            device_id=right,
            device_id_type=MESH,
        )

    def terms_for(head, step):
        return plane(lax.rem(z + (NZ - way(head)) * (step + 1), NZ))

    def sum_copy(head, which, step, src):
        return pltpu.make_async_remote_copy(
            src_ref=src,
            dst_ref=land.at[head, which, step],
            send_sem=sum_s.at[head, which, step],
            recv_sem=sum_r.at[head, which, step],
            device_id=neighbour(head),
            device_id_type=MESH,
        )

    def sum_first(head):
        for which in range(2):
            src = dkv_ref.at[head, which, :, terms_for(head, 0), :]
            sum_copy(head, which, 0, src).start()

    def sum_next(head, which, step):
        slot = land.at[head, which, step - 1]
        sum_copy(head, which, step - 1, slot).wait_recv()
        own = dkv_ref[head, which, :, terms_for(head, step), :]
        slot[...] = (own.astype(F32) + slot[...].astype(F32)).astype(BF16)

        def send_on():
            sum_copy(head, which, step, slot).start()

        if isinstance(step, int):
            if step < NZ - 1:
                send_on()
        else:
            pl.when(step < NZ - 1)(send_on)

    code = dot_nt(pick_wide, jnp.broadcast_to(doc_ref[...] + 1, (HD, ROWS)).astype(BF16))
    slot, lane = iota((256, HD), 0), iota((256, HD), 1)
    code = jnp.where(lane == lax.rem(me, 4) * CAP + lax.rem(slot, WIDE), code, 0.0).astype(BF16)
    sel = ((row // WIDE == col // WIDE) & (lax.rem(row, WIDE) == CAP)).astype(BF16)
    mix = message_from_wide()
    keys_pack(0, dot(sel, code), mix)
    pl.semaphore_wait(barrier, NG + 1)
    keys_start(0)
    keys_pack(1, None, mix)
    for load in loads:
        load.wait()
    for piece in (0, 1):
        rows_pack(piece)

    keys_unpack(0)
    total = recv0[0, 0, 2]
    for s in range(1, NG):
        total = total + recv0[0, s, 2]
    meta_ref[z] = total

    heads = (0, 1, 2, 3)
    for step in range(NZ - 1):
        for which in range(2):
            for head in heads:
                if step > 0:
                    gather_copy(head, which, step - 1).wait_recv()
                gather_copy(head, which, step).start()
        if step > 0:
            meta_copy(step - 1).wait_recv()
        meta_copy(step).start()
        if step == 0:
            keys_start(1)
        if step < PIECES:
            if step >= 2:
                rows_pack(step)
            rows_start(step)
        mask_block(meta_ref, bias, z, lax.rem(z - step + NZ, NZ))
        if step == 4:
            keys_unpack(1)
        if step >= 5:
            rows_unpack(step - 5) if step == 5 else None
    for which in range(2):
        for head in heads:
            gather_copy(SET + head, which, 0).start()
    meta_copy(NZ - 2).wait_recv()
    mask_block(meta_ref, bias, z, lax.rem(z + 1, NZ))
    for which in range(2):
        for head in heads:
            gather_copy(head, which, NZ - 2).wait_recv()

    refs = (kv_ref, qu_ref, gu_ref, ou_ref, dqu_ref, dkv_ref, bias, p_ref, ds_ref)

    def hop_of(event):
        pair = lax.rem(event, 2) * 2
        return 1 + event // 4, lax.rem(event // 2, 2), (pair, pair + 1)

    def first_heads(i, carry):
        def between(at):
            step, which, pair = hop_of(7 * i + at)
            for head in pair:
                gather_copy(SET + head, which, step - 1).wait_recv()

                @pl.when(step < NZ - 1)
                def _():
                    gather_copy(SET + head, which, step).start()

        attend_head(i, *refs, between)
        sum_first(i)
        between(4)

        @pl.when(i >= 1)
        def _():
            rows_unpack(i)

        between(5)

        @pl.when(lax.rem(i, 2) == 1)
        def _():
            results_start(i // 2)

        between(6)
        return carry

    lax.fori_loop(0, SET, first_heads, 0)

    def other_heads(i, carry):
        def between(at):
            step, which, pair = hop_of(7 * i + at)
            for head in pair:
                sum_next(head, which, step)

        attend_head(i + SET, *refs, between)
        sum_first(i + SET)
        between(4)
        between(5)

        @pl.when(lax.rem(i, 2) == 1)
        def _():
            results_start(2 + i // 2)

        between(6)
        return carry

    lax.fori_loop(0, SET, other_heads, 0)
    beside = {
        1: lambda: terms_start(0),
        6: lambda: results_unpack(0),
        10: lambda: results_unpack(1),
        18: lambda: terms_unpack(0),
    }
    for event in range(4 * (NZ - 1)):
        step, which, pair = 1 + event // 4, event // 2 % 2, event % 2 * 2
        for head in (pair, pair + 1):
            sum_next(SET + head, which, step)
        if event in beside:
            beside[event]()
    terms_start(1)
    for piece in (2, 3):
        results_unpack(piece)
    for store in stores:
        store.start()

    def ring_sent(step, carry):
        for which in range(2):
            for head in range(KVH):
                gather_copy(head, which, step).wait_send()
                sum_copy(head, which, step, land.at[head, which, step]).wait_send()
        meta_copy(step).wait_send()
        return carry

    lax.fori_loop(0, NZ - 1, ring_sent, 0)
    exchange_wait_send(dkv_send.at[0], dkv_s.at[0])
    for part in range(SETS):
        exchange_wait_send(send0.at[part], kv_s.at[part])
    for piece in range(PIECES):
        exchange_wait_send(send.at[piece], res_s.at[piece])
    terms_unpack(1)
    exchange_wait_send(dkv_send.at[1], dkv_s.at[1])
    for store in stores:
        store.wait()


def copy_kernel(*refs):
    srcs, dsts, held, into, out_of = refs[:4], refs[4:8], refs[8:12], refs[12], refs[13]
    loads, stores = [], []
    for src, dst, buf in zip(srcs, dsts, held):
        for part in range(4):
            rows, n = pl.ds(part * 32, 32), len(loads)
            loads.append(pltpu.make_async_copy(src.at[rows], buf.at[rows], into.at[n]))
            stores.append(pltpu.make_async_copy(buf.at[rows], dst.at[rows], out_of.at[n]))
    for load in loads:
        load.start()
    for load, store in zip(loads, stores):
        load.wait()
        store.start()
    for store in stores:
        store.wait()


def per_device(query, key_states, value_states, out_grad, target_group, document):
    vmem = pl.BlockSpec(memory_space=pltpu.VMEM)
    anywhere = pl.BlockSpec(memory_space=pl.ANY)
    dma = pltpu.SemaphoreType.DMA
    group = target_group.reshape(1, ROWS)
    doc = document.reshape(1, ROWS)
    kv_shape = (KVH, 2, 2, NZ * HALF, HD)
    heads_shape = (HEADS, SLOTS, HD)
    piece_shape = (PIECES, NG, CAP, UNITS, HD)
    message_shape = (SETS, NG, 3, 16, HD)
    out_shape = [
        jax.ShapeDtypeStruct((ROWS, HEADS * HD), BF16),
        jax.ShapeDtypeStruct((ROWS, HEADS * HD), BF16),
        jax.ShapeDtypeStruct((ROWS, KVH * HD), BF16),
        jax.ShapeDtypeStruct((ROWS, KVH * HD), BF16),
    ]
    result = pl.pallas_call(
        whole_kernel,
        out_shape=out_shape,
        in_specs=[anywhere, vmem, vmem, anywhere, vmem, vmem],
        out_specs=[anywhere, anywhere, vmem, vmem],
        scratch_shapes=[
            pltpu.VMEM((ROWS, HEADS * HD), BF16),
            pltpu.VMEM((ROWS, HEADS * HD), BF16),
            pltpu.VMEM((ROWS, HEADS * HD), BF16),
            pltpu.VMEM((ROWS, HEADS * HD), BF16),
            dma((2,)), dma((2,)),
            pltpu.VMEM(kv_shape, BF16),
            pltpu.VMEM((NZ, 16, HD), BF16),
            pltpu.VMEM(heads_shape, BF16),
            pltpu.VMEM(heads_shape, BF16),
            pltpu.VMEM(heads_shape, BF16),
            pltpu.VMEM(heads_shape, BF16),
            pltpu.VMEM(kv_shape, BF16),
            pltpu.VMEM((KEYS, LANES), F32),
            pltpu.VMEM((KEYS, LANES), BF16),
            pltpu.VMEM((KEYS, LANES), BF16),
            pltpu.VMEM(message_shape, BF16),
            pltpu.VMEM(message_shape, BF16),
            pltpu.VMEM(piece_shape, BF16),
            pltpu.VMEM(piece_shape, BF16),
            pltpu.VMEM(message_shape, BF16),
            pltpu.VMEM(message_shape, BF16),
            pltpu.VMEM(piece_shape, BF16),
            pltpu.VMEM((KVH, 2, NZ - 1, 2, HALF, HD), BF16),
            dma((SETS,)), dma((SETS,)), dma((SETS,)),
            dma((PIECES,)), dma((PIECES,)), dma((PIECES,)),
            dma((SETS,)), dma((SETS,)), dma((SETS,)),
            dma((PIECES,)), dma((PIECES,)), dma((PIECES,)),
            dma((KVH, 2, NZ - 1)), dma((KVH, 2, NZ - 1)),
            dma((KVH, 2, NZ - 1)), dma((KVH, 2, NZ - 1)),
            dma((NZ - 1,)), dma((NZ - 1,)),
        ],
        compiler_params=pltpu.CompilerParams(
            collective_id=0, has_side_effects=True, vmem_limit_bytes=VMEM_LIMIT
        ),
        name="whole",
    )(query, key_states, value_states, out_grad, group, doc)
    return tuple(
        pl.pallas_call(
            copy_kernel,
            out_shape=out_shape,
            in_specs=[anywhere] * 4,
            out_specs=[anywhere] * 4,
            scratch_shapes=[pltpu.VMEM(shape.shape, BF16) for shape in out_shape]
            + [dma((16,)), dma((16,))],
            name="place_outputs",
        )(*result)
    )


def solution(mesh):
    rows = P(("dp", "seq"), None)
    line = P(("dp", "seq"))
    return jax.shard_map(
        per_device,
        mesh=mesh,
        in_specs=(rows, rows, rows, rows, line, line),
        out_specs=(rows, rows, rows, rows),
        check_vma=False,
    )
```

```python
import math

import jax
import jax.numpy as jnp
from jax import lax
from jax.experimental import pallas as pl
from jax.experimental.pallas import tpu as pltpu
from jax.sharding import PartitionSpec as P

HD = 128
NX, NZ, NS = 4, 8, 8
NG = NX * NS
CAP = 5
SLOTS = NG * CAP
HALF = SLOTS // 2
KEYS = NZ * SLOTS
HEADS, KVH, RATIO = 32, 8, 4
UNITS = 16
PIECES = 4
ROWS = 128
BLK = 16
SET = KVH // 2
SETS = 2
WIDE = 8
LANES = RATIO * SLOTS
SPLIT = 256
INV_ROOT = 1.0 / math.sqrt(HD)
MESH = pl.DeviceIdType.MESH
BF16 = jnp.bfloat16
F32 = jnp.float32
VMEM_LIMIT = 56 * 1024 * 1024


def iota(shape, dim):
    return lax.broadcasted_iota(jnp.int32, shape, dim)


def dot(a, b):
    return lax.dot_general(a, b, (((1,), (0,)), ((), ())), preferred_element_type=F32)


def dot_nt(a, b):
    return lax.dot_general(a, b, (((1,), (1,)), ((), ())), preferred_element_type=F32)


def place():
    dp, seq = lax.axis_index("dp"), lax.axis_index("seq")
    return dp // NZ, lax.rem(dp, NZ), seq


def plane_device(x, z, seq, step):
    to = lax.rem(x * NS + seq + step * 11, NG)
    return to, (lax.div(to, NS) * NZ + z, lax.rem(to, NS))


def slot_matrix(group_ref, width):
    across = jnp.broadcast_to(group_ref[...], (ROWS, ROWS)).astype(F32)
    down = across.T
    earlier = (across == down) & (iota((ROWS, ROWS), 0) < iota((ROWS, ROWS), 1))
    rank = jnp.sum(earlier.astype(F32), axis=0, keepdims=True)
    slot = across[:1] * width + rank
    return (iota((NG * width, ROWS), 0).astype(F32) == slot).astype(BF16)


def transposed(matrix):
    return matrix.astype(F32).T.astype(BF16)


def swap_tiles(swap, tiles):
    mixed = dot(swap, jnp.concatenate(tiles, axis=0)).astype(BF16)
    return [mixed[i * 16 : (i + 1) * 16] for i in range(mixed.shape[0] // 16)]


def greet(x, z, seq, ring):
    barrier = pltpu.get_barrier_semaphore()

    def signal(step, carry):
        _, device = plane_device(x, z, seq, step)
        pl.semaphore_signal(barrier, inc=1, device_id=device, device_id_type=MESH)
        return carry

    for device in ring:
        pl.semaphore_signal(barrier, inc=1, device_id=device, device_id_type=MESH)
    lax.fori_loop(1, NG, signal, 0)
    return barrier


def exchange_start(x, z, seq, send, recv, send_sem, recv_sem, own_sem):
    me = x * NS + seq

    def one(step, carry):
        to, device = plane_device(x, z, seq, step)
        pltpu.make_async_remote_copy(
            src_ref=send.at[to],
            dst_ref=recv.at[me],
            send_sem=send_sem,
            recv_sem=recv_sem,
            device_id=device,
            device_id_type=MESH,
        ).start()
        return carry

    lax.fori_loop(1, NG, one, 0)
    pltpu.make_async_copy(send.at[me], recv.at[me], own_sem).start()


def exchange_wait_recv(recv, recv_sem, own_sem):
    pltpu.make_async_copy(recv.at[pl.ds(0, NG - 1)], recv.at[pl.ds(0, NG - 1)], recv_sem).wait()
    pltpu.make_async_copy(recv.at[0], recv.at[0], own_sem).wait()


def exchange_wait_send(send, send_sem):
    pltpu.make_async_copy(send.at[pl.ds(0, NG - 1)], send.at[pl.ds(0, NG - 1)], send_sem).wait()


def token_tiles(ref, piece, block):
    return [ref[piece, t // CAP, t % CAP] for t in range(block * BLK, block * BLK + BLK)]


def put_tiles(ref, piece, block, tiles):
    for i, tile in enumerate(tiles):
        t = block * BLK + i
        ref[piece, t // CAP, t % CAP] = tile


def message_from_wide():
    out, src = iota((192, 256), 0), iota((192, 256), 1)
    group, row, unit = out // 48, lax.rem(out, 48) // 8, lax.rem(out, 8)
    return (src == unit * 32 + group * 8 + row).astype(BF16)


def units_from_message(block):
    out, src = iota((128, 192), 0), iota((128, 192), 1)
    slot = block * BLK + lax.rem(out, BLK) - first_message(block) * CAP
    return (src == (slot // CAP) * 48 + lax.rem(slot, CAP) * 8 + out // BLK).astype(BF16)


def first_message(block):
    return block * BLK // CAP


def message_from_units(four):
    out, src = iota((192, 256), 0), iota((192, 256), 1)
    row, unit = lax.rem(out, 48) // 8, lax.rem(out, 8)
    slot = four * 4 * CAP + (out // 48) * CAP + row - (four * 4 * CAP // BLK) * BLK
    return ((src == unit * 32 + slot) & (row < CAP)).astype(BF16)


def query_slots(rows):
    lane = iota((rows, LANES), 1)
    return (lane // (RATIO * HALF)) * HALF + lax.rem(lane, HALF)


def query_codes(meta):
    expand = (iota((HD, LANES), 0) == lax.rem(query_slots(HD), 20)).astype(BF16)
    own = iota((16, LANES), 0) == 8 + query_slots(16) // 20
    return jnp.sum(jnp.where(own, dot(meta, expand), 0.0), axis=0, keepdims=True)


def mask_block(meta_ref, bias, z, zk):
    tq = query_slots(1)
    code_q = query_codes(meta_ref[z])
    order_q = (tq // 40) * 320 + z * 40 + lax.rem(tq, 40)
    slot, lane = iota((SLOTS, HD), 0), iota((SLOTS, HD), 1)
    spread = (8 + iota((SLOTS, 16), 0) // 20 == iota((SLOTS, 16), 1)).astype(BF16)
    picked = jnp.where(lane == lax.rem(slot, 20), dot(spread, meta_ref[zk]), 0.0).astype(BF16)
    code_k = dot(picked, jnp.ones((HD, HD), BF16))
    order_k = (slot // 40) * 320 + zk * 40 + lax.rem(slot, 40)
    for half in range(2):
        rows = slice(half * HALF, (half + 1) * HALF)
        at_row = pl.multiple_of(half * NZ * HALF + zk * HALF, BLK)
        for at in range(0, LANES, HD):
            cols = slice(at, at + HD)
            ok = (
                (code_k[rows] == code_q[:, cols])
                & (code_k[rows] > 0.5)
                & (order_k[rows] <= order_q[:, cols])
            )
            bias[pl.ds(at_row, HALF), cols] = jnp.where(ok, 0.0, -1e30)


def attend_head(
    c, kv_ref, q_ref, g_ref, o_ref, dq_ref, dkv_ref, bias, p_ref, ds_ref, between
):
    log_scale = INV_ROOT * math.log2(math.e)

    def rows_of(ref):
        return jnp.concatenate(
            [
                ref[c * RATIO + h, half * HALF : (half + 1) * HALF, :]
                for half in range(2)
                for h in range(RATIO)
            ],
            axis=0,
        )

    q, g = rows_of(q_ref), rows_of(g_ref)
    k = kv_ref[c, 0].reshape(KEYS, HD)
    v = kv_ref[c, 1].reshape(KEYS, HD)
    kt, vt = k.T, v.T
    blocks = ((0, SPLIT, KEYS // 2), (SPLIT, 2 * SPLIT, KEYS), (2 * SPLIT, LANES, KEYS))
    outs, dqs = [], []

    def products(i):
        lo, hi, n = blocks[i]
        return dot_nt(k[:n], q[lo:hi]), dot_nt(v[:n], g[lo:hi])

    def softmax(i, s, dp):
        lo, hi, n = blocks[i]
        s = s * log_scale + bias[:n, lo:hi]
        e = jnp.exp2(s - jnp.max(s, axis=0, keepdims=True))
        scale = 1.0 / jnp.sum(e, axis=0, keepdims=True)
        delta = jnp.sum(e * dp, axis=0, keepdims=True) * scale
        p = e * scale
        low, ds = p.astype(BF16), (p * (dp - delta)).astype(BF16)
        p_ref[:n, lo:hi] = low
        ds_ref[:n, lo:hi] = ds
        return low, ds

    def results(i, low, ds):
        n = blocks[i][2]
        outs.append(dot(vt[:, :n], low).astype(BF16).T)
        dqs.append((dot(kt[:, :n], ds) * INV_ROOT).astype(BF16).T)

    first, second = products(0), products(1)
    done = softmax(0, *first)
    between(0)
    third = products(2)
    after = softmax(1, *second)
    results(0, *done)
    between(1)
    done = softmax(2, *third)
    results(1, *after)
    between(2)
    results(2, *done)
    n = KEYS // 2
    for half, lo in ((0, 0), (1, SPLIT)):
        rows = slice(half * n, (half + 1) * n)
        dkv_ref[c, 0, half] = (dot(ds_ref[rows, lo:], q[lo:]) * INV_ROOT).astype(BF16)
        dkv_ref[c, 1, half] = dot(p_ref[rows, lo:], g[lo:]).astype(BF16)
        if half == 0:
            between(3)
    out, dq = jnp.concatenate(outs, axis=0), jnp.concatenate(dqs, axis=0)
    for half in range(2):
        for h in range(RATIO):
            rows = slice((half * RATIO + h) * HALF, (half * RATIO + h + 1) * HALF)
            o_ref[c * RATIO + h, half * HALF : (half + 1) * HALF, :] = out[rows]
            dq_ref[c * RATIO + h, half * HALF : (half + 1) * HALF, :] = dq[rows]


def whole_kernel(
    q_in, k_ref, v_ref, g_in, group_ref, doc_ref,
    out_hbm, qg_hbm, kg_ref, vg_ref,
    q_ref, g_ref, out_ref, qg_ref, load_sem, store_sem,
    kv_ref, meta_ref, qu_ref, gu_ref, ou_ref, dqu_ref, dkv_ref,
    bias, p_ref, ds_ref,
    send0, recv0, send, recv, dkv_send, back0, back, land,
    kv_s, kv_r, kv_o, row_s, row_r, row_o, dkv_s, dkv_r, dkv_o, res_s, res_r, res_o,
    ring_s, ring_r, sum_s, sum_r, meta_s, meta_r,
):
    x, z, seq = place()
    me = x * NS + seq
    right = (x * NZ + lax.rem(z + 1, NZ), seq)
    left = (x * NZ + lax.rem(z + NZ - 1, NZ), seq)
    loads = [
        pltpu.make_async_copy(src, dst, load_sem.at[i])
        for i, (src, dst) in enumerate(((q_in, q_ref), (g_in, g_ref)))
    ]
    stores = [
        pltpu.make_async_copy(src, dst, store_sem.at[i])
        for i, (src, dst) in enumerate(((out_ref, out_hbm), (qg_ref, qg_hbm)))
    ]
    barrier = greet(x, z, seq, (left, right))
    for load in loads:
        load.start()

    pick = slot_matrix(group_ref, CAP)
    pick_wide = slot_matrix(group_ref, WIDE)
    row, col = iota((256, 256), 0), iota((256, 256), 1)
    swap = (col == lax.rem(row, 16) * 16 + row // 16).astype(BF16)

    def rows_pack(piece):
        cols = slice(piece * 1024, (piece + 1) * 1024)
        packed = [dot(pick, part[:, cols]).astype(BF16) for part in (q_ref, g_ref)]
        for block in range(SLOTS // BLK):
            rows = slice(block * BLK, (block + 1) * BLK)
            tiles = [part[rows, at * HD : (at + 1) * HD] for part in packed for at in range(8)]
            put_tiles(send, piece, block, swap_tiles(swap, tiles))

    def rows_start(piece):
        exchange_start(
            x, z, seq, send.at[piece], recv.at[piece],
            row_s.at[piece], row_r.at[piece], row_o.at[piece],
        )

    def rows_unpack(piece):
        exchange_wait_recv(recv.at[piece], row_r.at[piece], row_o.at[piece])
        for block in range(SLOTS // BLK):
            tiles = swap_tiles(swap, token_tiles(recv, piece, block))
            rows = slice(block * BLK, (block + 1) * BLK)
            for unit in range(8):
                qu_ref[piece * 8 + unit, rows, :] = tiles[unit]
                gu_ref[piece * 8 + unit, rows, :] = tiles[8 + unit]

    def results_start(piece):
        exchange_wait_send(send.at[piece], row_s.at[piece])
        for block in range(SLOTS // BLK):
            rows = slice(block * BLK, (block + 1) * BLK)
            tiles = [ou_ref[piece * 8 + unit, rows, :] for unit in range(8)]
            tiles += [dqu_ref[piece * 8 + unit, rows, :] for unit in range(8)]
            put_tiles(send, piece, block, swap_tiles(swap, tiles))
        exchange_start(
            x, z, seq, send.at[piece], back.at[piece],
            res_s.at[piece], res_r.at[piece], res_o.at[piece],
        )

    def results_unpack(piece):
        exchange_wait_recv(back.at[piece], res_r.at[piece], res_o.at[piece])
        pick_t = transposed(pick)
        parts = [[] for _ in range(UNITS)]
        for block in range(SLOTS // BLK):
            tiles = swap_tiles(swap, token_tiles(back, piece, block))
            for unit in range(UNITS):
                parts[unit].append(tiles[unit])
        for unit in range(UNITS):
            rows = jnp.concatenate(parts[unit], axis=0)
            at = (piece * 8 + unit % 8) * HD
            (out_ref, qg_ref)[unit // 8][:, at : at + HD] = dot(pick_t, rows).astype(BF16)

    def keys_pack(part, extra, mix):
        packed = []
        for unit in range(8):
            at = (part * SET + unit // 2) * HD
            rows = dot(pick_wide, (k_ref, v_ref)[unit % 2][:, at : at + HD])
            if extra is not None:
                rows = rows + jnp.where(me // 4 == unit, extra, 0.0)
            packed.append(rows.astype(BF16))
        for four in range(NG // 4):
            rows = slice(four * 32, (four + 1) * 32)
            tiles = swap_tiles(mix, [part_rows[rows] for part_rows in packed])
            for i, tile in enumerate(tiles):
                send0[part, four * 4 + i // 3, i % 3] = tile

    def keys_start(part):
        exchange_start(
            x, z, seq, send0.at[part], recv0.at[part],
            kv_s.at[part], kv_r.at[part], kv_o.at[part],
        )

    def keys_unpack(part):
        exchange_wait_recv(recv0.at[part], kv_r.at[part], kv_o.at[part])
        here = pl.multiple_of(z * HALF, BLK)
        for block in range(SLOTS // BLK):
            first = first_message(block)
            tiles = [recv0[part, first + i // 3, i % 3] for i in range(12)]
            tiles = swap_tiles(units_from_message(block), tiles)
            half, at = block // 5, (block % 5) * BLK
            for unit in range(8):
                kv_ref[part * SET + unit // 2, unit % 2, half, pl.ds(here + at, BLK), :] = tiles[
                    unit
                ]

    def terms_start(part):
        for four in range(NG // 4):
            lo = four * 4 * CAP // BLK * BLK
            tiles = []
            for unit in range(8):
                for at in (lo, lo + BLK):
                    half, in_half = at // HALF, at % HALF
                    tiles.append(
                        land[part * SET + unit // 2, unit % 2, NZ - 2, half, in_half : in_half + BLK, :]
                    )
            tiles = swap_tiles(message_from_units(four), tiles)
            for i, tile in enumerate(tiles):
                dkv_send[part, four * 4 + i // 3, i % 3] = tile
        exchange_start(
            x, z, seq, dkv_send.at[part], back0.at[part],
            dkv_s.at[part], dkv_r.at[part], dkv_o.at[part],
        )

    def terms_unpack(part):
        exchange_wait_recv(back0.at[part], dkv_r.at[part], dkv_o.at[part])
        pick_t = transposed(pick_wide)
        mix = transposed(message_from_wide())
        parts = [[] for _ in range(8)]
        for four in range(NG // 4):
            tiles = [back0[part, four * 4 + i // 3, i % 3] for i in range(12)]
            tiles = swap_tiles(mix, tiles)
            for unit in range(8):
                parts[unit] += tiles[2 * unit : 2 * unit + 2]
        for unit in range(8):
            rows = jnp.concatenate(parts[unit], axis=0)
            at = (part * SET + unit // 2) * HD
            (kg_ref, vg_ref)[unit % 2][:, at : at + HD] = dot(pick_t, rows).astype(BF16)

    def plane(index):
        return pl.ds(pl.multiple_of(index * HALF, BLK), HALF)

    def way(head):
        return 1 + lax.rem(head, 2) * (NZ - 2)

    def neighbour(head):
        return (x * NZ + lax.rem(z + way(head), NZ), seq)

    def gather_copy(head, which, step):
        owner = lax.rem(z + (NZ - way(head)) * step, NZ)
        block = kv_ref.at[head, which, :, plane(owner), :]
        return pltpu.make_async_remote_copy(
            src_ref=block,
            dst_ref=block,
            send_sem=ring_s.at[head, which, step],
            recv_sem=ring_r.at[head, which, step],
            device_id=neighbour(head),
            device_id_type=MESH,
        )

    def meta_copy(step):
        owner = lax.rem(z - step + NZ, NZ)
        return pltpu.make_async_remote_copy(
            src_ref=meta_ref.at[owner],
            dst_ref=meta_ref.at[owner],
            send_sem=meta_s.at[step],
            recv_sem=meta_r.at[step],
            device_id=right,
            device_id_type=MESH,
        )

    def terms_for(head, step):
        return plane(lax.rem(z + (NZ - way(head)) * (step + 1), NZ))

    def sum_copy(head, which, step, src):
        return pltpu.make_async_remote_copy(
            src_ref=src,
            dst_ref=land.at[head, which, step],
            send_sem=sum_s.at[head, which, step],
            recv_sem=sum_r.at[head, which, step],
            device_id=neighbour(head),
            device_id_type=MESH,
        )

    def sum_first(head):
        for which in range(2):
            src = dkv_ref.at[head, which, :, terms_for(head, 0), :]
            sum_copy(head, which, 0, src).start()

    def sum_next(head, which, step):
        slot = land.at[head, which, step - 1]
        sum_copy(head, which, step - 1, slot).wait_recv()
        own = dkv_ref[head, which, :, terms_for(head, step), :]
        slot[...] = (own.astype(F32) + slot[...].astype(F32)).astype(BF16)

        def send_on():
            sum_copy(head, which, step, slot).start()

        if isinstance(step, int):
            if step < NZ - 1:
                send_on()
        else:
            pl.when(step < NZ - 1)(send_on)

    code = dot_nt(pick_wide, jnp.broadcast_to(doc_ref[...] + 1, (HD, ROWS)).astype(BF16))
    slot, lane = iota((256, HD), 0), iota((256, HD), 1)
    code = jnp.where(lane == lax.rem(me, 4) * CAP + lax.rem(slot, WIDE), code, 0.0).astype(BF16)
    sel = ((row // WIDE == col // WIDE) & (lax.rem(row, WIDE) == CAP)).astype(BF16)
    mix = message_from_wide()
    keys_pack(0, dot(sel, code), mix)
    pl.semaphore_wait(barrier, NG + 1)
    keys_start(0)
    keys_pack(1, None, mix)
    for load in loads:
        load.wait()
    for piece in (0, 1):
        rows_pack(piece)

    keys_unpack(0)
    total = recv0[0, 0, 2]
    for s in range(1, NG):
        total = total + recv0[0, s, 2]
    meta_ref[z] = total

    heads = (0, 1, 2, 3)
    for step in range(NZ - 1):
        for which in range(2):
            for head in heads:
                if step > 0:
                    gather_copy(head, which, step - 1).wait_recv()
                gather_copy(head, which, step).start()
        if step > 0:
            meta_copy(step - 1).wait_recv()
        meta_copy(step).start()
        if step == 0:
            keys_start(1)
        if step < PIECES:
            if step >= 2:
                rows_pack(step)
            rows_start(step)
        mask_block(meta_ref, bias, z, lax.rem(z - step + NZ, NZ))
        if step == 4:
            keys_unpack(1)
        if step >= 5:
            rows_unpack(step - 5) if step == 5 else None
    for which in range(2):
        for head in heads:
            gather_copy(SET + head, which, 0).start()
    meta_copy(NZ - 2).wait_recv()
    mask_block(meta_ref, bias, z, lax.rem(z + 1, NZ))
    for which in range(2):
        for head in heads:
            gather_copy(head, which, NZ - 2).wait_recv()

    refs = (kv_ref, qu_ref, gu_ref, ou_ref, dqu_ref, dkv_ref, bias, p_ref, ds_ref)

    def hop_of(event):
        pair = lax.rem(event, 2) * 2
        return 1 + event // 4, lax.rem(event // 2, 2), (pair, pair + 1)

    def first_heads(i, carry):
        def between(at):
            step, which, pair = hop_of(7 * i + at)
            for head in pair:
                gather_copy(SET + head, which, step - 1).wait_recv()

                @pl.when(step < NZ - 1)
                def _():
                    gather_copy(SET + head, which, step).start()

        attend_head(i, *refs, between)
        sum_first(i)
        between(4)

        @pl.when(i >= 1)
        def _():
            rows_unpack(i)

        between(5)

        @pl.when(lax.rem(i, 2) == 1)
        def _():
            results_start(i // 2)

        between(6)
        return carry

    lax.fori_loop(0, SET, first_heads, 0)

    def other_heads(i, carry):
        def between(at):
            step, which, pair = hop_of(7 * i + at)
            for head in pair:
                sum_next(head, which, step)

        attend_head(i + SET, *refs, between)
        sum_first(i + SET)
        between(4)
        between(5)

        @pl.when(lax.rem(i, 2) == 1)
        def _():
            results_start(2 + i // 2)

        between(6)
        return carry

    lax.fori_loop(0, SET, other_heads, 0)
    beside = {
        1: lambda: terms_start(0),
        6: lambda: results_unpack(0),
        10: lambda: results_unpack(1),
        18: lambda: terms_unpack(0),
    }
    for event in range(4 * (NZ - 1)):
        step, which, pair = 1 + event // 4, event // 2 % 2, event % 2 * 2
        for head in (pair, pair + 1):
            sum_next(SET + head, which, step)
        if event in beside:
            beside[event]()
    terms_start(1)
    for piece in (2, 3):
        results_unpack(piece)
    for store in stores:
        store.start()

    def ring_sent(step, carry):
        for which in range(2):
            for head in range(KVH):
                gather_copy(head, which, step).wait_send()
                sum_copy(head, which, step, land.at[head, which, step]).wait_send()
        meta_copy(step).wait_send()
        return carry

    lax.fori_loop(0, NZ - 1, ring_sent, 0)
    exchange_wait_send(dkv_send.at[0], dkv_s.at[0])
    for part in range(SETS):
        exchange_wait_send(send0.at[part], kv_s.at[part])
    for piece in range(PIECES):
        exchange_wait_send(send.at[piece], res_s.at[piece])
    terms_unpack(1)
    exchange_wait_send(dkv_send.at[1], dkv_s.at[1])
    for store in stores:
        store.wait()


def copy_kernel(*refs):
    srcs, dsts, held, into, out_of = refs[:4], refs[4:8], refs[8:12], refs[12], refs[13]
    loads, stores = [], []
    for src, dst, buf in zip(srcs, dsts, held):
        for part in range(4):
            rows, n = pl.ds(part * 32, 32), len(loads)
            loads.append(pltpu.make_async_copy(src.at[rows], buf.at[rows], into.at[n]))
            stores.append(pltpu.make_async_copy(buf.at[rows], dst.at[rows], out_of.at[n]))
    for load in loads:
        load.start()
    for load, store in zip(loads, stores):
        load.wait()
        store.start()
    for store in stores:
        store.wait()


def per_device(query, key_states, value_states, out_grad, target_group, document):
    vmem = pl.BlockSpec(memory_space=pltpu.VMEM)
    anywhere = pl.BlockSpec(memory_space=pl.ANY)
    dma = pltpu.SemaphoreType.DMA
    group = target_group.reshape(1, ROWS)
    doc = document.reshape(1, ROWS)
    kv_shape = (KVH, 2, 2, NZ * HALF, HD)
    heads_shape = (HEADS, SLOTS, HD)
    piece_shape = (PIECES, NG, CAP, UNITS, HD)
    message_shape = (SETS, NG, 3, 16, HD)
    out_shape = [
        jax.ShapeDtypeStruct((ROWS, HEADS * HD), BF16),
        jax.ShapeDtypeStruct((ROWS, HEADS * HD), BF16),
        jax.ShapeDtypeStruct((ROWS, KVH * HD), BF16),
        jax.ShapeDtypeStruct((ROWS, KVH * HD), BF16),
    ]
    result = pl.pallas_call(
        whole_kernel,
        out_shape=out_shape,
        in_specs=[anywhere, vmem, vmem, anywhere, vmem, vmem],
        out_specs=[anywhere, anywhere, vmem, vmem],
        scratch_shapes=[
            pltpu.VMEM((ROWS, HEADS * HD), BF16),
            pltpu.VMEM((ROWS, HEADS * HD), BF16),
            pltpu.VMEM((ROWS, HEADS * HD), BF16),
            pltpu.VMEM((ROWS, HEADS * HD), BF16),
            dma((2,)), dma((2,)),
            pltpu.VMEM(kv_shape, BF16),
            pltpu.VMEM((NZ, 16, HD), BF16),
            pltpu.VMEM(heads_shape, BF16),
            pltpu.VMEM(heads_shape, BF16),
            pltpu.VMEM(heads_shape, BF16),
            pltpu.VMEM(heads_shape, BF16),
            pltpu.VMEM(kv_shape, BF16),
            pltpu.VMEM((KEYS, LANES), F32),
            pltpu.VMEM((KEYS, LANES), BF16),
            pltpu.VMEM((KEYS, LANES), BF16),
            pltpu.VMEM(message_shape, BF16),
            pltpu.VMEM(message_shape, BF16),
            pltpu.VMEM(piece_shape, BF16),
            pltpu.VMEM(piece_shape, BF16),
            pltpu.VMEM(message_shape, BF16),
            pltpu.VMEM(message_shape, BF16),
            pltpu.VMEM(piece_shape, BF16),
            pltpu.VMEM((KVH, 2, NZ - 1, 2, HALF, HD), BF16),
            dma((SETS,)), dma((SETS,)), dma((SETS,)),
            dma((PIECES,)), dma((PIECES,)), dma((PIECES,)),
            dma((SETS,)), dma((SETS,)), dma((SETS,)),
            dma((PIECES,)), dma((PIECES,)), dma((PIECES,)),
            dma((KVH, 2, NZ - 1)), dma((KVH, 2, NZ - 1)),
            dma((KVH, 2, NZ - 1)), dma((KVH, 2, NZ - 1)),
            dma((NZ - 1,)), dma((NZ - 1,)),
        ],
        compiler_params=pltpu.CompilerParams(
            collective_id=0, has_side_effects=True, vmem_limit_bytes=VMEM_LIMIT
        ),
        name="whole",
    )(query, key_states, value_states, out_grad, group, doc)
    return tuple(
        pl.pallas_call(
            copy_kernel,
            out_shape=out_shape,
            in_specs=[anywhere] * 4,
            out_specs=[anywhere] * 4,
            scratch_shapes=[pltpu.VMEM(shape.shape, BF16) for shape in out_shape]
            + [dma((16,)), dma((16,))],
            name="place_outputs",
        )(*result)
    )


def solution(mesh):
    rows = P(("dp", "seq"), None)
    line = P(("dp", "seq"))
    return jax.shard_map(
        per_device,
        mesh=mesh,
        in_specs=(rows, rows, rows, rows, line, line),
        out_specs=(rows, rows, rows, rows),
        check_vma=False,
    )
```
